256 devices in a mesh: gx: 8 (over x, core), gy: 32 (over z, y).
Axes of the slice: x: 4, y: 4, z: 8, core: 2. Of those that a mesh axis runs over, the one named last changes fastest.
Arguments:
- hidden: bfloat16 [32, 512, 1280], P('gy', 'gx'), may hold values from -6 to 6
- lengths: int32 [32], P('gy'), may hold values from 4 to 16384, as said below
- sink_kv: bfloat16 [32, 2, 4, 1024], P('gy', None, None, 'gx'), may hold values from -12 to 12
- kv_cycle: bfloat16 [32, 2, 4608, 1024], P('gy', None, None, 'gx'), may hold values from -12 to 12
- w_qkv: bfloat16 [1280, 3, 1024], P('gy', None, 'gx'), may hold values from -0.15625 to 0.15625
- s_qk: float32 [1024], P('gx'), may hold values from 0.5 to 16
- w_out: bfloat16 [1024, 1280], P('gx', 'gy'), may hold values from -0.1875 to 0.1875
- alpha_attn: float32 [1280], replicated, may hold values from 0.05 to 0.8
- w_up: bfloat16 [1280, 5120], P('gy', 'gx'), may hold values from -0.15625 to 0.15625
- w_gate: bfloat16 [1280, 5120], P('gy', 'gx'), may hold values from -0.15625 to 0.15625
- s_up: float32 [5120], P('gx'), may hold values from 0.5 to 2
- s_gate: float32 [5120], P('gx'), may hold values from 0.5 to 2
- w_down: bfloat16 [5120, 1280], P('gx', 'gy'), may hold values from -0.078125 to 0.078125
- alpha_mlp: float32 [1280], replicated, may hold values from 0.05 to 0.8
Outputs:
- new_hidden: bfloat16 [32, 512, 1280], P('gy', 'gx')
- new_cycle: bfloat16 [32, 2, 4608, 1024], P('gy', None, None, 'gx')
The draws below stay inside these ranges and needn't reach their ends.
Inputs may be any that keep to these rules, and one draw needn't show every extreme that they name: `lengths`: exactly 8 requests, chosen by the seed, have 16384 cached positions; the others have fewer than 256.
All inputs are finite; a program needn't handle non-finite values.
Results may differ from the reference program's by a relative error of at most 0.012.
The reference program's roundings to bfloat16 on the way (of `queries`, `keys_new`, `values_new`, `attended`, `after_attn` and `active`) count: a program that leaves them out, or rounds other values in their place, can miss the bound.
Values may be sent and summed in bfloat16 or wider, within the bound.
A program may use at most 64 MiB of HBM per device.

```python
import math
import jax
import jax.numpy as jnp
from jax import lax

D = 1280
HD = 64
FF = 5120
HEADS = 16
HQ = 1024
NEW_TOK = 512
REQ = 32
SINK = 4
WINDOW = 4096
CYCLE = 4608
L_LONG = 16384
SHORT = 256


def scales(key):
    spread = jax.random.uniform(jax.random.fold_in(key, 1), (HEADS, HD), jnp.float32, -0.6931472, 0.6931472)
    result = jnp.exp(spread)
    return result


def cache_values(key, slots):
    scale_qk = scales(jax.random.fold_in(key, 99)).reshape(HEADS * HD)
    noise = jnp.clip(jax.random.normal(jax.random.fold_in(key, slots), (REQ, 2, slots, HEADS * HD), jnp.float32), -6.0, 6.0)
    factor = jnp.stack([scale_qk * 0.125, jnp.ones_like(scale_qk)])
    return (noise * factor[None, :, None, :]).astype(jnp.bfloat16)


def draw_lengths(key, part):
    order = jax.random.permutation(jax.random.fold_in(key, 11), REQ)
    shorter = jax.random.randint(jax.random.fold_in(key, 12), (REQ,), SINK, SHORT)
    return jnp.where(order < REQ // 4, L_LONG, shorter).astype(jnp.int32)


def draw_s_qk(key, part):
    return scales(jax.random.fold_in(key, 99)).reshape(HEADS * HD).astype(jnp.float32)


def draw_sink_kv(key, part):
    return cache_values(jax.random.fold_in(key, 21), SINK)


def draw_kv_cycle(key, part):
    return cache_values(jax.random.fold_in(key, 22), CYCLE)


def steps_of(rng, shape, split, low, top_value):
    def one(axis_at, parts):
        heights = jax.random.uniform(jax.random.fold_in(jax.random.fold_in(rng, 6), axis_at), (parts,), jnp.float32, low / len(split), top_value / len(split))
        return jnp.repeat(jnp.exp(heights), shape[axis_at] // parts).reshape((-1,) + (1,) * (len(shape) - axis_at - 1))

    loudness = one(*split[0])
    for cut in split[1:]:
        loudness = loudness * one(*cut)
    return loudness


def bell_draw(key, extent, width, bound, pieces=(), kind=jnp.bfloat16):
    array = jax.random.normal(key, extent, jnp.float32) * width
    if len(pieces) > 0:
        array = steps_of(key, extent, pieces, -0.22, 0.18) * array
    return jnp.clip(array, min=-bound, max=bound).astype(kind)


def setup_inputs(seed: int = 0) -> dict:
    splits = jax.random.split(jax.random.key(seed), 15)
    return {
        "hidden": bell_draw(splits[0], (REQ, NEW_TOK, D), 1.0, 6.0, ((0, 32), (1, 8))),
        "lengths": draw_lengths(jax.random.fold_in(splits[14], 71), 0),
        "sink_kv": draw_sink_kv(jax.random.fold_in(splits[14], 71), 0),
        "kv_cycle": draw_kv_cycle(jax.random.fold_in(splits[14], 71), 0),
        "w_qkv": bell_draw(splits[4], (D, 3, HQ), D ** -0.5, 0.15625, ((0, 32), (2, 8))),
        "s_qk": draw_s_qk(jax.random.fold_in(splits[14], 71), 0),
        "w_out": bell_draw(splits[6], (HQ, D), HQ ** -0.5, 0.1875, ((0, 8), (1, 32))),
        "alpha_attn": jnp.clip(jnp.exp(jax.random.uniform(splits[7], (D,), jnp.float32, math.log(0.05), math.log(0.8))), 0.05, 0.8),
        "w_up": bell_draw(splits[8], (D, FF), D ** -0.5, 0.15625, ((0, 32), (1, 8))),
        "w_gate": bell_draw(splits[9], (D, FF), D ** -0.5, 0.15625, ((0, 32), (1, 8))),
        "s_up": jnp.clip(jnp.exp(math.log(2.0) - 1.3862944 * jax.random.uniform(splits[10], (FF,), jnp.float32) ** steps_of(splits[10], (FF,), ((0, 8),), -0.2, 0.2)), 0.5, 2.0),
        "s_gate": jnp.clip(jnp.exp(math.log(2.0) - 1.3862944 * jax.random.uniform(splits[11], (FF,), jnp.float32) ** steps_of(splits[11], (FF,), ((0, 8),), -0.2, 0.2)), 0.5, 2.0),
        "w_down": bell_draw(splits[12], (FF, D), FF ** -0.5, 0.078125, ((0, 8), (1, 32))),
        "alpha_mlp": jnp.clip(jnp.exp(jax.random.uniform(splits[13], (D,), jnp.float32, math.log(0.05), math.log(0.8))), 0.05, 0.8),
    }


def rms_unit(values):
    return values * lax.rsqrt(lax.optimization_barrier(jnp.mean(values * values, axis=-1, keepdims=True)) + 1e-06)

def head_unit(values):
    return values * lax.rsqrt(lax.optimization_barrier(jnp.sum(values * values, axis=-1, keepdims=True)) + 1e-06)

def slot_positions(length, slot_ids):
    lagging = length + NEW_TOK - 1 - SINK - slot_ids
    filled = lagging >= 0
    wrapped = jnp.where(filled, lagging, 0) // CYCLE
    return (SINK + slot_ids + CYCLE * wrapped, filled)

def reference(hidden, lengths, sink_kv, kv_cycle, w_qkv, s_qk, w_out, alpha_attn, w_up, w_gate, s_up, s_gate, w_down, alpha_mlp):
    scale_qk = s_qk.reshape(HEADS, HD)
    factor = math.sqrt(HD)

    def one_request(operands):
        tokens, length, sink_rows, cached = operands
        projected = jnp.dot(tokens, w_qkv.reshape(D, 3 * HQ), preferred_element_type=jnp.float32).reshape(NEW_TOK, 3, HEADS, HD)
        queries = (head_unit(projected[:, 0]) * scale_qk).astype(jnp.bfloat16)
        keys_new = (head_unit(projected[:, 1]) * scale_qk).astype(jnp.bfloat16)
        values_new = projected[:, 2].astype(jnp.bfloat16)
        start_slot = (length - SINK) % CYCLE
        targets = (start_slot + jnp.arange(NEW_TOK, dtype=jnp.int32)) % CYCLE
        updated = cached.at[0, targets].set(keys_new.reshape(NEW_TOK, HQ))
        updated = updated.at[1, targets].set(values_new.reshape(NEW_TOK, HQ))
        positions, filled = slot_positions(length, jnp.arange(CYCLE, dtype=jnp.int32))
        moments = length + jnp.arange(NEW_TOK, dtype=jnp.int32)
        visible = filled[None, :] & (positions[None, :] <= moments[:, None]) & (positions[None, :] > moments[:, None] - WINDOW)
        visible = jnp.concatenate([jnp.ones((NEW_TOK, SINK), jnp.int32) > 0, visible], axis=1)
        all_keys = jnp.concatenate([sink_rows[0], updated[0]], axis=0).reshape(SINK + CYCLE, HEADS, HD)
        all_values = jnp.concatenate([sink_rows[1], updated[1]], axis=0).reshape(SINK + CYCLE, HEADS, HD)
        scores = jnp.einsum('qhd,khd->qhk', queries.astype(jnp.float32), all_keys.astype(jnp.float32)) * factor
        scores = jnp.where(visible[:, None, :], scores, -1e+30)
        highest = lax.optimization_barrier(jnp.max(scores, axis=-1, keepdims=True))
        weights = jnp.where(visible[:, None, :], jnp.exp(scores - highest), 0.0)
        totals = lax.optimization_barrier(jnp.sum(weights, axis=-1))
        rounded = lax.optimization_barrier(weights.astype(jnp.bfloat16)).astype(jnp.float32)
        gathered = jnp.einsum('qhk,khd->qhd', rounded, all_values.astype(jnp.float32))
        attended = (gathered / totals[:, :, None]).astype(jnp.bfloat16).reshape(NEW_TOK, HQ)
        attn_mixed = jnp.dot(attended, w_out, preferred_element_type=jnp.float32)
        residual = tokens.astype(jnp.float32)
        after_attn = rms_unit(residual + alpha_attn * (rms_unit(attn_mixed) - residual)).astype(jnp.bfloat16)
        up_branch = jnp.dot(after_attn, w_up, preferred_element_type=jnp.float32) * s_up
        gate_branch = jnp.dot(after_attn, w_gate, preferred_element_type=jnp.float32) * s_gate
        active = (up_branch * jax.nn.silu(gate_branch)).astype(jnp.bfloat16)
        lowered = jnp.dot(active, w_down, preferred_element_type=jnp.float32)
        after_wide = after_attn.astype(jnp.float32)
        result = rms_unit(after_wide + alpha_mlp * (rms_unit(lowered) - after_wide)).astype(jnp.bfloat16)
        return (result, updated)
    new_hidden, new_cycle = lax.map(one_request, (hidden, lengths, sink_kv, kv_cycle))
    return (new_hidden, new_cycle)
```

```python
import functools

import jax
import jax.numpy as jnp
from jax import lax
from jax.experimental import pallas as pl
from jax.experimental.pallas import tpu as pltpu
from jax.sharding import PartitionSpec as P

MESH = pl.DeviceIdType.MESH
BF16 = jnp.bfloat16
F32 = jnp.float32

XC, YC, ZC = 4, 4, 8
D = 1280
HQ = 128
FF = 640
TOK = 512
OWN = 64
PAIR = 128
SHARD = 40
PLANE = SHARD * YC
SINK = 4
WINDOW = 4096
CYCLE = 4608
LONG = 16384
HEAD = 3056
TAIL = 2544
OLD = CYCLE - HEAD + TAIL
NEW_AT = OLD + 16
CHUNK = 256
CHUNKS = 17
KEYS = 3 * PAIR + CHUNK * CHUNKS
FIRST = 13
AWAY = -1e30
EARLY = (0, 1)
LATE = (2, 3, 4, 5)
RIGHT_LAST = (1, 2, 5)


def dot(a, b):
    return jnp.dot(a, b, preferred_element_type=F32)


def dot_nt(a, b):
    return lax.dot_general(a, b, (((1,), (1,)), ((), ())), preferred_element_type=F32)


def rms_unit(values):
    return values * lax.rsqrt(jnp.mean(values * values, axis=-1, keepdims=True) + 1e-06)


def lanes(shape):
    return lax.broadcasted_iota(jnp.int32, shape, len(shape) - 1)


def rows_of(shape):
    return lax.broadcasted_iota(jnp.int32, shape, len(shape) - 2)


def layer_kernel(
    lengths,
    hidden,
    sinks,
    cached,
    w_qkv,
    s_qk,
    w_out,
    alpha_attn,
    w_up,
    w_gate,
    s_up,
    s_gate,
    w_down,
    alpha_mlp,
    result,
    fresh,
    g_qkv,
    g_out,
    g_ff,
    g_down,
    edge_a,
    edge_b,
    tokens,
    keys,
    values,
    queries,
    scores,
    partial,
    kept,
    to_sib,
    from_sib,
    to_owner,
    from_peer,
    after,
    local_sem,
    tok_send,
    tok_recv,
    shard_send,
    shard_recv,
    ring_send,
    ring_recv,
    quarter_send,
    quarter_recv,
    sib_send,
    sib_recv,
    sum_send,
    sum_recv,
):
    gx = lax.axis_index("gx")
    gy = lax.axis_index("gy")
    x, c = gx // 2, lax.rem(gx, 2)
    z, y = gy // YC, lax.rem(gy, YC)

    def device(dx=0, other=False, dz=0, dy=0):
        core = 1 - c if other else c
        return (
            lax.rem(x + dx, XC) * 2 + core,
            lax.rem(z + dz, ZC) * YC + lax.rem(y + dy, YC),
        )

    sibling = device(other=True)
    along_x = {d: device(dx=d) for d in (1, 2, 3)}
    along_y = {d: device(dy=d) for d in (1, 2, 3)}
    right, left = device(dz=1), device(dz=ZC - 1)
    everyone = [sibling, *along_x.values(), *along_y.values(), right, left]
    gate_sem = pltpu.get_barrier_semaphore()
    for peer in everyone:
        pl.semaphore_signal(gate_sem, inc=1, device_id=peer, device_id_type=MESH)

    sent = []

    def remote(src, dst, send, recv, to):
        return pltpu.make_async_remote_copy(
            src_ref=src, dst_ref=dst, send_sem=send, recv_sem=recv, device_id=to, device_id_type=MESH
        )

    def go(copy):
        copy.start()
        sent.append(copy)

    def block_of(g):
        return pl.ds(pl.multiple_of(g * OWN, OWN), OWN)

    own_in = pltpu.make_async_copy(hidden.at[0], tokens.at[block_of(gx)], local_sem.at[0])
    own_in.start()
    loads = []
    for kind, store in ((0, keys), (1, values)):
        for n, (src, at, count) in enumerate(
            ((HEAD, 0, CYCLE - HEAD), (0, CYCLE - HEAD, TAIL))
        ):
            loads.append(
                pltpu.make_async_copy(
                    cached.at[0, kind, pl.ds(src, count)],
                    store.at[pl.ds(at, count), pl.ds(0, HQ)],
                    local_sem.at[1 + 2 * kind + n],
                )
            )
    for load in loads:
        load.start()

    odd = lax.rem(y, 2)
    main_rows = pl.ds(
        pl.multiple_of(z * PLANE + (y // 2) * (2 * SHARD) + odd * 48, 16), 32
    )

    def cut(wide):
        main = jnp.where(odd == 1, wide[8:40], wide[0:32]).astype(BF16)
        edge = jnp.concatenate([wide[32:40], wide[0:8]], axis=0).astype(BF16)
        return main, edge

    main, edge = cut(w_qkv[...].astype(F32))
    g_qkv[main_rows, :] = main
    edge_a[y] = edge

    pl.semaphore_wait(gate_sem, len(everyone))

    def shard_copies(n, src_dst):
        return [
            remote(src_dst, src_dst, shard_send.at[n, d - 1], shard_recv.at[n, d - 1], along_y[d])
            for d in (1, 2, 3)
        ]

    first_wave = shard_copies(0, g_qkv.at[main_rows]) + shard_copies(1, edge_a.at[y])
    for copy in first_wave:
        go(copy)

    own_in.wait()

    def token_copy(buffer, phase, d):
        piece = buffer.at[block_of(gx)]
        to = sibling if d == 0 else along_x[d]
        return remote(piece, piece, tok_send.at[phase, d], tok_recv.at[phase, d], to)

    def token_pass_on(buffer, phase, d):
        came = block_of(lax.rem(x + XC - d, XC) * 2 + c)
        direct = remote(
            buffer.at[came], buffer.at[came], tok_send.at[phase, d], tok_recv.at[phase, d], along_x[d]
        )
        direct.wait_recv()
        go(
            remote(
                buffer.at[came],
                buffer.at[came],
                tok_send.at[phase, 3 + d],
                tok_recv.at[phase, 3 + d],
                sibling,
            )
        )

    def token_from_sibling(buffer, phase, d):
        block = buffer.at[block_of(lax.rem(x + XC - d, XC) * 2 + 1 - c)]
        n = 0 if d == 0 else 3 + d
        remote(block, block, tok_send.at[phase, n], tok_recv.at[phase, n], sibling).wait_recv()

    for d in (1, 3, 2, 0):
        go(token_copy(tokens, 0, d))

    def one_hot(n):
        return jnp.where(rows_of((n, n)) == lanes((n, n)), 1.0, 0.0).astype(BF16)

    turned = dot_nt(one_hot(SHARD), w_out[...])
    main, edge = cut(turned)
    g_out[main_rows, :] = main
    edge_b[y, :, 0:HQ] = edge
    up_wide = w_up[...].astype(F32)
    gate_wide = w_gate[...].astype(F32)
    for b in range(5):
        cols = slice(b * HQ, b * HQ + HQ)
        main, edge = cut(jnp.concatenate([up_wide[:, cols], gate_wide[:, cols]], axis=1))
        g_ff[b, main_rows, :] = main
        edge_b[y, :, HQ + 256 * b : HQ + 256 * (b + 1)] = edge
    main, edge = cut(dot_nt(one_hot(SHARD), w_down[...]))
    g_down[main_rows, :] = main
    edge_b[y, :, HQ + 2 * FF :] = edge
    second_wave = (
        shard_copies(2, edge_b.at[y])
        + shard_copies(3, g_ff.at[:, main_rows])
        + shard_copies(4, g_out.at[main_rows])
        + shard_copies(5, g_down.at[main_rows])
    )
    for copy in second_wave:
        go(copy)

    def plane(zz):
        return pl.ds(pl.multiple_of(zz * PLANE, 32), PLANE)

    def part_ref(part, zz):
        if part == 0:
            return g_qkv.at[plane(zz), pl.ds(0, HQ)]
        if part == 1:
            return g_qkv.at[plane(zz), pl.ds(HQ, 2 * HQ)]
        if part == 2:
            return g_ff.at[y, plane(zz)]
        if part == 3:
            return g_ff.at[4, plane(zz)]
        if part == 4:
            return g_out.at[plane(zz)]
        return g_down.at[plane(zz)]

    def last_step(part, way):
        return 4 if (part in RIGHT_LAST) == (way == 0) else 3

    def ring_copy(part, way, step, arriving):
        back = step if arriving else step - 1
        zz = lax.rem(z + ZC - back, ZC) if way == 0 else lax.rem(z + back, ZC)
        piece = part_ref(part, zz)
        return remote(
            piece,
            piece,
            ring_send.at[part, way, step - 1],
            ring_recv.at[part, way, step - 1],
            right if way == 0 else left,
        ), zz

    def quarter_copies(way, step, zz):
        n = step - 1 if way == 0 else 4 + step - 1
        piece = g_ff.at[y, plane(zz)]
        return [
            remote(piece, piece, quarter_send.at[n, d - 1], quarter_recv.at[n, d - 1], along_y[d])
            for d in (1, 2, 3)
        ]

    def ring_stage(parts, step):
        for part in parts:
            for way in (0, 1):
                if 1 <= step - 1 <= last_step(part, way):
                    copy, zz = ring_copy(part, way, step - 1, True)
                    copy.wait_recv()
                if step <= last_step(part, way):
                    go(ring_copy(part, way, step, False)[0])
                if 1 <= step - 1 <= last_step(part, way) and part == 2:
                    for copy in quarter_copies(way, step - 1, zz):
                        go(copy)

    def merge(ref, edges, col, width):
        for pair in (0, 1):
            low = edges[2 * pair, :, col : col + width].astype(F32)
            high = edges[2 * pair + 1, :, col : col + width].astype(F32)
            at = pl.multiple_of(z * PLANE + pair * 2 * SHARD + 32, 16)
            ref[pl.ds(at, 16), :] = jnp.concatenate([low[0:8], high[8:16]], axis=0).astype(BF16)

    def rows_from(d):
        yy = lax.rem(y + YC - d, YC)
        at = z * PLANE + (yy // 2) * (2 * SHARD) + lax.rem(yy, 2) * 48
        return yy, pl.ds(pl.multiple_of(at, 16), 32)

    def shard_arrived(n, ref_of):
        for d in (1, 2, 3):
            yy, rows = rows_from(d)
            piece = ref_of(yy, rows)
            remote(
                piece, piece, shard_send.at[n, d - 1], shard_recv.at[n, d - 1], along_y[d]
            ).wait_recv()

    shard_arrived(0, lambda yy, rows: g_qkv.at[rows])
    shard_arrived(1, lambda yy, rows: edge_a.at[yy])
    merge(g_qkv, edge_a, 0, 3 * HQ)
    ring_stage(EARLY, 1)

    length = lengths[0]

    def key_bias(n, carry):
        at = pl.multiple_of(n * PAIR, PAIR)
        row = rows_of((PAIR, HQ)) + at
        slot = jnp.where(row < CYCLE - HEAD, row + HEAD, row - (CYCLE - HEAD))
        lag = length - 1 - SINK - slot
        turns = (
            jnp.where(lag >= CYCLE, 1, 0)
            + jnp.where(lag >= 2 * CYCLE, 1, 0)
            + jnp.where(lag >= 3 * CYCLE, 1, 0)
        )
        held = SINK + slot + CYCLE * turns
        old = (lag >= 0) & (held >= length - WINDOW) & (row < OLD + 12)
        seen = old | ((row >= OLD + 12) & (row < NEW_AT + TOK))
        keys[pl.ds(at, PAIR), HQ : 2 * HQ] = jnp.where(seen, 0.0, AWAY).astype(BF16)
        values[pl.ds(at, PAIR), HQ : 2 * HQ] = jnp.ones((PAIR, HQ), BF16)
        return carry

    lax.fori_loop(0, KEYS // PAIR, key_bias, 0)
    spare = KEYS - NEW_AT - TOK
    for kind, store in ((0, keys), (1, values)):
        store[OLD:NEW_AT, 0:HQ] = sinks[kind]
        store[NEW_AT + TOK :, 0:HQ] = jnp.zeros((spare, HQ), BF16)

    shard_arrived(2, lambda yy, rows: edge_b.at[yy])
    shard_arrived(3, lambda yy, rows: g_ff.at[:, rows])
    shard_arrived(4, lambda yy, rows: g_out.at[rows])
    shard_arrived(5, lambda yy, rows: g_down.at[rows])
    merge(g_out, edge_b, 0, HQ)
    for b in range(5):
        merge(g_ff.at[b], edge_b, HQ + 256 * b, 256)
    merge(g_down, edge_b, HQ + 2 * FF, FF)
    ring_stage(LATE, 1)
    ring_stage(EARLY, 2)
    for d in (1, 3):
        token_pass_on(tokens, 0, d)
    ring_stage(EARLY, 3)
    token_pass_on(tokens, 0, 2)
    ring_stage(LATE, 2)
    ring_stage(EARLY, 4)
    for d in (0, 1, 2, 3):
        token_from_sibling(tokens, 0, d)
    for step in (4,):
        for part in EARLY:
            for way in (0, 1):
                if last_step(part, way) == step:
                    ring_copy(part, way, step, True)[0].wait_recv()
    for load in loads:
        load.wait()

    low_head = lanes((PAIR, HQ)) < 64

    def head_unit(v):
        squares = v * v
        low = jnp.sum(jnp.where(low_head, squares, 0.0), axis=-1, keepdims=True)
        high = jnp.sum(jnp.where(low_head, 0.0, squares), axis=-1, keepdims=True)
        return v * jnp.where(low_head, lax.rsqrt(low + 1e-06), lax.rsqrt(high + 1e-06))

    def project(n, carry):
        at = pl.multiple_of(n * PAIR, PAIR)
        qkv = dot(tokens[pl.ds(at, PAIR), :], g_qkv[...])
        scale = s_qk[...]
        q = (head_unit(qkv[:, 0:HQ]) * scale).astype(BF16)
        queries[pl.ds(at, PAIR), :] = (q.astype(F32) * 8.0).astype(BF16)
        k = (head_unit(qkv[:, HQ : 2 * HQ]) * scale).astype(BF16)
        v = qkv[:, 2 * HQ :].astype(BF16)
        to = pl.ds(pl.multiple_of(NEW_AT + at, 16), PAIR)
        keys[to, 0:HQ] = k
        values[to, 0:HQ] = v
        fresh[0, 0, pl.ds(at, PAIR), :] = k
        fresh[0, 1, pl.ds(at, PAIR), :] = v
        return carry

    lax.fori_loop(0, TOK // PAIR, project, 0)
    ring_stage(LATE, 3)

    def own_half(ref):
        return ref[pl.ds(pl.multiple_of(c * OWN, OWN), OWN), :]

    def other_half(ref):
        return ref[pl.ds(pl.multiple_of((1 - c) * OWN, OWN), OWN), :]

    def sib_copy(phase, k):
        return remote(
            to_sib.at[phase, k],
            from_sib.at[phase, k],
            sib_send.at[phase, k],
            sib_recv.at[phase, k],
            sibling,
        )

    def owner_copy(phase, k, d):
        to = (lax.rem(x + d, XC) * 2 + c, gy)
        return remote(
            to_owner.at[phase, k],
            from_peer.at[phase, k],
            sum_send.at[phase, k],
            sum_recv.at[phase, k],
            to,
        )

    def give_halves(phase, k):
        kept[phase, k] = own_half(partial)
        to_sib[phase, k] = other_half(partial).astype(BF16)
        sib_copy(phase, k).start()

    def chip_sum(phase, k):
        sib_copy(phase, k).wait_recv()
        return kept[phase, k] + from_sib[phase, k].astype(F32)

    def send_sum(phase, k, d):
        to_owner[phase, k] = chip_sum(phase, k).astype(BF16)
        owner_copy(phase, k, d).start()

    query_row = jnp.where(
        rows_of((2 * PAIR, CHUNK)) >= PAIR, rows_of((2 * PAIR, CHUNK)) - PAIR, rows_of((2 * PAIR, CHUNK))
    )
    key_col = lanes((2 * PAIR, CHUNK))

    def far_first(k):
        return jnp.where(k == 0, 2, jnp.where(k == 1, 1, jnp.where(k == 2, 3, 0)))

    def attend(k, carry):
        block = lax.rem(x + far_first(k), XC)
        at = pl.multiple_of(block * PAIR, PAIR)
        q = queries[pl.ds(at, PAIR), :]
        zero = jnp.zeros_like(q)
        both = jnp.concatenate([jnp.where(low_head, q, zero), jnp.where(low_head, zero, q)], axis=0)
        lhs = jnp.concatenate([both, jnp.ones((2 * PAIR, HQ), BF16)], axis=1)
        top = jnp.full((2 * PAIR, HQ), -jnp.inf, F32)
        for n in range(CHUNKS):
            s = dot_nt(lhs, keys[pl.ds(at + n * CHUNK, CHUNK), :])
            if n == 0:
                s = jnp.where(key_col >= query_row + FIRST, s, AWAY)
            if n == CHUNKS - 1:
                s = jnp.where(key_col + n * CHUNK <= query_row + NEW_AT, s, AWAY)
            scores[:, n * CHUNK : (n + 1) * CHUNK] = s
            top = jnp.maximum(top, jnp.maximum(s[:, 0:HQ], s[:, HQ:]))
        highest = jnp.max(top, axis=-1, keepdims=True)
        weighted = jnp.zeros((2 * PAIR, 2 * HQ), F32)
        for n in range(CHUNKS):
            w = jnp.exp(scores[:, n * CHUNK : (n + 1) * CHUNK] - highest).astype(BF16)
            weighted += dot(w, values[pl.ds(at + n * CHUNK, CHUNK), :])
        mean = weighted[:, 0:HQ] / weighted[:, HQ:]
        attended = jnp.where(low_head, mean[0:PAIR], mean[PAIR:]).astype(BF16)
        partial[...] = dot_nt(attended, g_out[...])
        give_halves(0, k)

        @pl.when(k > 0)
        def _():
            send_sum(0, k - 1, far_first(k - 1))

        return carry

    def finish(parts, step):
        for part in parts:
            for way in (0, 1):
                if last_step(part, way) == step:
                    copy, zz = ring_copy(part, way, step, True)
                    copy.wait_recv()
                    if part == 2:
                        for copy in quarter_copies(way, step, zz):
                            go(copy)

    ring_stage(LATE, 4)
    finish((4,), 4)
    lax.fori_loop(0, 4, attend, 0)
    finish((2, 3, 5), 4)

    total = chip_sum(0, 3)
    for k, d in ((0, 2), (1, 1), (2, 3)):
        owner_copy(0, k, d).wait_recv()
        total = total + from_peer[0, k].astype(F32)
    residual = tokens[block_of(gx), :].astype(F32)
    updated = rms_unit(residual + alpha_attn[...] * (rms_unit(total) - residual)).astype(BF16)
    after[block_of(gx), :] = updated
    for d in (0, 1, 3, 2):
        go(token_copy(after, 1, d))

    for n in range(7):
        back = n + 1 if n < 4 else ZC - (n - 3)
        zz = lax.rem(z + ZC - back, ZC)
        for d in (1, 2, 3):
            piece = g_ff.at[lax.rem(y + YC - d, YC), plane(zz)]
            remote(
                piece, piece, quarter_send.at[n, d - 1], quarter_recv.at[n, d - 1], along_y[d]
            ).wait_recv()

    def near_first(k):
        return jnp.where(k == 0, 0, jnp.where(k == 1, 1, jnp.where(k == 2, 3, 2)))

    def feed(k):
        block = lax.rem(x + XC - near_first(k), XC)
        rows = after[pl.ds(pl.multiple_of(block * PAIR, PAIR), PAIR), :]
        total_low = jnp.zeros((PAIR, D), F32)
        acts = []
        for b in range(5):
            both = dot(rows, g_ff[b])
            cols = slice(b * HQ, b * HQ + HQ)
            up = both[:, 0:HQ] * s_up[:, cols]
            gate = both[:, HQ:] * s_gate[:, cols]
            acts.append((up * (gate / (1.0 + jnp.exp(-gate)))).astype(BF16))
        active = jnp.concatenate(acts, axis=1)
        partial[...] = dot_nt(active, g_down[...])
        give_halves(1, k)

    def back_of(k):
        return lax.rem(XC - near_first(k), XC)

    token_from_sibling(after, 1, 0)

    def feed_step(k, carry):
        @pl.when(k == 1)
        def _():
            for d in (1, 3):
                token_pass_on_only(d)
            token_from_sibling(after, 1, 1)

        @pl.when(k == 2)
        def _():
            token_pass_on_only(2)
            token_from_sibling(after, 1, 3)

        @pl.when(k == 3)
        def _():
            token_from_sibling(after, 1, 2)

        feed(k)

        @pl.when(k >= 2)
        def _():
            send_sum(1, k - 1, back_of(k - 1))

        return carry

    def pass_on_copy(d):
        came = block_of(lax.rem(x + XC - d, XC) * 2 + c)
        return remote(
            after.at[came], after.at[came], tok_send.at[1, 3 + d], tok_recv.at[1, 3 + d], sibling
        )

    def token_pass_on_only(d):
        came = block_of(lax.rem(x + XC - d, XC) * 2 + c)
        remote(
            after.at[came], after.at[came], tok_send.at[1, d], tok_recv.at[1, d], along_x[d]
        ).wait_recv()
        pass_on_copy(d).start()

    lax.fori_loop(0, 4, feed_step, 0)
    send_sum(1, 3, 2)
    lowered = chip_sum(1, 0)
    for k in (1, 2, 3):
        owner_copy(1, k, 1).wait_recv()
        lowered = lowered + from_peer[1, k].astype(F32)
    wide = updated.astype(F32)
    result[0] = rms_unit(wide + alpha_mlp[...] * (rms_unit(lowered) - wide)).astype(BF16)

    for copy in sent:
        copy.wait_send()
    for k in range(4):
        for phase in (0, 1):
            sib_copy(phase, k).wait_send()
    for k, d in ((0, 2), (1, 1), (2, 3)):
        owner_copy(0, k, d).wait_send()
    for k, d in ((1, 3), (2, 1), (3, 2)):
        owner_copy(1, k, d).wait_send()
    for d in (1, 2, 3):
        pass_on_copy(d).wait_send()


def per_device(
    hidden,
    lengths,
    sink_kv,
    kv_cycle,
    w_qkv,
    s_qk,
    w_out,
    alpha_attn,
    w_up,
    w_gate,
    s_up,
    s_gate,
    w_down,
    alpha_mlp,
):
    sinks = jnp.concatenate([kv_cycle[0, :, TAIL : TAIL + 12], sink_kv[0]], axis=1)
    vmem = pl.BlockSpec(memory_space=pltpu.VMEM)
    anywhere = pl.BlockSpec(memory_space=pl.ANY)
    dma = pltpu.SemaphoreType.DMA
    result, fresh = pl.pallas_call(
        layer_kernel,
        out_shape=(
            jax.ShapeDtypeStruct((1, OWN, D), BF16),
            jax.ShapeDtypeStruct((1, 2, TOK, HQ), BF16),
        ),
        in_specs=[
            pl.BlockSpec(memory_space=pltpu.SMEM),
            anywhere,
            vmem,
            anywhere,
            vmem,
            vmem,
            vmem,
            vmem,
            vmem,
            vmem,
            vmem,
            vmem,
            vmem,
            vmem,
        ],
        out_specs=(vmem, vmem),
        scratch_shapes=[
            pltpu.VMEM((D, 3 * HQ), BF16),
            pltpu.VMEM((D, HQ), BF16),
            pltpu.VMEM((5, D, 2 * HQ), BF16),
            pltpu.VMEM((D, FF), BF16),
            pltpu.VMEM((YC, 16, 3 * HQ), BF16),
            pltpu.VMEM((YC, 16, HQ + 3 * FF), BF16),
            pltpu.VMEM((TOK, D), BF16),
            pltpu.VMEM((KEYS, 2 * HQ), BF16),
            pltpu.VMEM((KEYS, 2 * HQ), BF16),
            pltpu.VMEM((TOK, HQ), BF16),
            pltpu.VMEM((2 * PAIR, CHUNK * CHUNKS), F32),
            pltpu.VMEM((PAIR, D), F32),
            pltpu.VMEM((2, 4, OWN, D), F32),
            pltpu.VMEM((2, 4, OWN, D), BF16),
            pltpu.VMEM((2, 4, OWN, D), BF16),
            pltpu.VMEM((2, 4, OWN, D), BF16),
            pltpu.VMEM((2, 4, OWN, D), BF16),
            pltpu.VMEM((TOK, D), BF16),
            dma((5,)),
            dma((2, 7)),
            dma((2, 7)),
            dma((6, 3)),
            dma((6, 3)),
            dma((6, 2, 4)),
            dma((6, 2, 4)),
            dma((7, 3)),
            dma((7, 3)),
            dma((2, 4)),
            dma((2, 4)),
            dma((2, 4)),
            dma((2, 4)),
        ],
        compiler_params=pltpu.CompilerParams(
            collective_id=0, has_side_effects=True, vmem_limit_bytes=56 * 2**20
        ),
    )(
        lengths,
        hidden,
        sinks,
        kv_cycle,
        w_qkv.reshape(SHARD, 3 * HQ),
        s_qk.reshape(1, HQ),
        w_out,
        alpha_attn.reshape(1, D),
        w_up,
        w_gate,
        s_up.reshape(1, FF),
        s_gate.reshape(1, FF),
        w_down,
        alpha_mlp.reshape(1, D),
    )
    start = lax.rem(lengths[0] - SINK, CYCLE)
    new_cycle = lax.dynamic_update_slice(kv_cycle, fresh, (0, 0, start, 0))
    return result, new_cycle


def solution(mesh):
    return jax.shard_map(
        per_device,
        mesh=mesh,
        in_specs=(
            P("gy", "gx", None),
            P("gy"),
            P("gy", None, None, "gx"),
            P("gy", None, None, "gx"),
            P("gy", None, "gx"),
            P("gx"),
            P("gx", "gy"),
            P(),
            P("gy", "gx"),
            P("gy", "gx"),
            P("gx"),
            P("gx"),
            P("gx", "gy"),
            P(),
        ),
        out_specs=(P("gy", "gx", None), P("gy", None, None, "gx")),
        check_vma=False,
    )
```

```python
import functools

import jax
import jax.numpy as jnp
from jax import lax
from jax.experimental import pallas as pl
from jax.experimental.pallas import tpu as pltpu
from jax.sharding import PartitionSpec as P

MESH = pl.DeviceIdType.MESH
BF16 = jnp.bfloat16
F32 = jnp.float32

XC, YC, ZC = 4, 4, 8
D = 1280
HQ = 128
FF = 640
TOK = 512
OWN = 64
PAIR = 128
SHARD = 40
PLANE = SHARD * YC
SINK = 4
WINDOW = 4096
CYCLE = 4608
LONG = 16384
HEAD = 3056
TAIL = 2544
OLD = CYCLE - HEAD + TAIL
NEW_AT = OLD + 16
CHUNK = 256
CHUNKS = 17
KEYS = 3 * PAIR + CHUNK * CHUNKS
FIRST = 13
AWAY = -1e30
DOWN, REST, FRONT = 0, 1, 2
OUT = 2
GATE_FRONT = 256
GATE_REST = FF - GATE_FRONT
RIGHT_LAST = (DOWN,)


def dot(a, b):
    return jnp.dot(a, b, preferred_element_type=F32)


def dot_nt(a, b):
    return lax.dot_general(a, b, (((1,), (1,)), ((), ())), preferred_element_type=F32)


def rms_unit(values):
    return values * lax.rsqrt(jnp.mean(values * values, axis=-1, keepdims=True) + 1e-06)


def lanes(shape):
    return lax.broadcasted_iota(jnp.int32, shape, len(shape) - 1)


def rows_of(shape):
    return lax.broadcasted_iota(jnp.int32, shape, len(shape) - 2)


def layer_kernel(
    lengths,
    hidden,
    sinks,
    cached,
    w_qkv,
    s_qk,
    w_out,
    alpha_attn,
    w_up,
    w_gate,
    s_up,
    s_gate,
    w_down,
    alpha_mlp,
    result,
    fresh,
    l_qkv,
    l_out,
    l_down,
    l_rest,
    l_front,
    g_qkv,
    g_out,
    g_ff,
    g_down,
    tokens,
    keys,
    values,
    queries,
    even_scores,
    odd_scores,
    attended,
    partial,
    kept,
    to_sib,
    from_sib,
    to_owner,
    from_peer,
    after,
    local_sem,
    tok_send,
    tok_recv,
    qkv_send,
    qkv_recv,
    out_send,
    out_recv,
    shard_send,
    shard_recv,
    ring_send,
    ring_recv,
    quarter_send,
    quarter_recv,
    sib_send,
    sib_recv,
    sum_send,
    sum_recv,
):
    gx = lax.axis_index("gx")
    gy = lax.axis_index("gy")
    x, c = gx // 2, lax.rem(gx, 2)
    z, y = gy // YC, lax.rem(gy, YC)

    def device(dx=0, other=False, dz=0, dy=0):
        core = 1 - c if other else c
        return (
            lax.rem(x + dx, XC) * 2 + core,
            lax.rem(z + dz, ZC) * YC + lax.rem(y + dy, YC),
        )

    sibling = device(other=True)
    along_x = {d: device(dx=d) for d in (1, 2, 3)}
    along_y = {d: device(dy=d) for d in (1, 2, 3)}
    right, left = device(dz=1), device(dz=ZC - 1)
    along_z = [device(dz=d) for d in range(1, ZC)]
    everyone = [sibling, *along_x.values(), *along_y.values(), *along_z]
    gate_sem = pltpu.get_barrier_semaphore()
    for peer in everyone:
        pl.semaphore_signal(gate_sem, inc=1, device_id=peer, device_id_type=MESH)

    sent = []

    def remote(src, dst, send, recv, to):
        return pltpu.make_async_remote_copy(
            src_ref=src, dst_ref=dst, send_sem=send, recv_sem=recv, device_id=to, device_id_type=MESH
        )

    def go(copy):
        copy.start()
        sent.append(copy)

    def block_of(g):
        return pl.ds(pl.multiple_of(g * OWN, OWN), OWN)

    own_in = pltpu.make_async_copy(hidden.at[0], tokens.at[block_of(gx)], local_sem.at[0])
    own_in.start()
    loads = []
    for kind, store in ((0, keys), (1, values)):
        for n, (src, at, count) in enumerate(
            ((HEAD, 0, CYCLE - HEAD), (0, CYCLE - HEAD, TAIL + 16))
        ):
            loads.append(
                pltpu.make_async_copy(
                    cached.at[0, kind, pl.ds(src, count)],
                    store.at[pl.ds(at, count), pl.ds(0, HQ)],
                    local_sem.at[1 + 2 * kind + n],
                )
            )
    for load in loads:
        load.start()

    mine = [
        (w_qkv, l_qkv.at[z, y]),
        (w_up, l_front.at[z, y, :, pl.ds(0, FF)]),
        (w_gate.at[:, pl.ds(0, GATE_FRONT)], l_front.at[z, y, :, pl.ds(FF, GATE_FRONT)]),
        (w_gate.at[:, pl.ds(GATE_FRONT, GATE_REST)], l_rest.at[z, y, :, pl.ds(0, GATE_REST)]),
        (w_down, l_down.at[z, y]),
        (w_out, l_out.at[z, y]),
    ]
    mine = [pltpu.make_async_copy(a, b, local_sem.at[5 + n]) for n, (a, b) in enumerate(mine)]
    for copy in mine:
        copy.start()

    def over_y(piece, sends, recvs):
        return [remote(piece, piece, sends(d - 1), recvs(d - 1), along_y[d]) for d in (1, 2, 3)]

    def qkv_over_z(dz, arriving=False):
        zz = lax.rem(z + ZC - dz, ZC) if arriving else z
        piece = l_qkv.at[zz, y]
        return remote(piece, piece, qkv_send.at[0, dz], qkv_recv.at[0, dz], device(dz=dz))

    def qkv_over_y(dz):
        piece = l_qkv.at[lax.rem(z + ZC - dz, ZC), y]
        return over_y(piece, lambda n: qkv_send.at[1 + n, dz], lambda n: qkv_recv.at[1 + n, dz])

    def out_over_z(dz, arriving=False):
        piece = l_out.at[lax.rem(z + ZC - dz, ZC) if arriving else z]
        return remote(piece, piece, out_send.at[dz], out_recv.at[dz], device(dz=dz))

    def from_y(d):
        return lax.rem(y + YC - d, YC)

    def shard_over_y(part):
        piece = (l_down, l_rest, l_out)[part].at[z, y]
        return over_y(piece, lambda n: shard_send.at[part, n], lambda n: shard_recv.at[part, n])

    def shard_arrived(part):
        for d in (1, 2, 3):
            piece = (l_down, l_rest, l_out)[part].at[z, from_y(d)]
            remote(
                piece, piece, shard_send.at[part, d - 1], shard_recv.at[part, d - 1], along_y[d]
            ).wait_recv()

    def last_step(part, way):
        return 4 if (part in RIGHT_LAST) == (way == 0) else 3

    def ring_copy(part, way, step, arriving):
        back = step if arriving else step - 1
        zz = lax.rem(z + ZC - back, ZC) if way == 0 else lax.rem(z + back, ZC)
        piece = (l_down.at[zz], l_rest.at[zz], l_front.at[zz, y])[part]
        return remote(
            piece,
            piece,
            ring_send.at[part, way, step - 1],
            ring_recv.at[part, way, step - 1],
            right if way == 0 else left,
        )

    def front_over_y(n):
        piece = l_front.at[lax.rem(z + ZC - n, ZC), y]
        return over_y(piece, lambda m: quarter_send.at[n, m], lambda m: quarter_recv.at[n, m])

    def ring_stage(part, step):
        for way in (0, 1):
            if 1 <= step - 1 <= last_step(part, way):
                ring_copy(part, way, step - 1, True).wait_recv()
            if step <= last_step(part, way):
                go(ring_copy(part, way, step, False))

    pl.semaphore_wait(gate_sem, len(everyone))
    mine[0].wait()
    for dz in (1, 7, 2, 6, 3, 5, 4):
        go(qkv_over_z(dz))
    mine[5].wait()
    for copy in (*shard_over_y(OUT), *qkv_over_y(0)):
        go(copy)
    for n in (3, 4):
        mine[n].wait()
    for part in (DOWN, REST):
        for copy in shard_over_y(part):
            go(copy)

    own_in.wait()

    def held_by(d, other=False):
        core = 1 - c if other else c
        return lax.rem(x + XC - d, XC) * 2 + core

    def token_piece(g):
        return tokens.at[block_of(g)]

    def out_piece(g):
        return g_out.at[g]

    def attended_piece(n):
        return lambda g: attended.at[g, pl.ds(pl.multiple_of(n * PAIR, PAIR), PAIR)]

    def x_copy(piece, phase, d):
        to = sibling if d == 0 else along_x[d]
        return remote(piece(gx), piece(gx), tok_send.at[phase, d], tok_recv.at[phase, d], to)

    def x_pass_copy(piece, phase, d):
        block = piece(held_by(d))
        return remote(block, block, tok_send.at[phase, 3 + d], tok_recv.at[phase, 3 + d], sibling)

    def x_pass_on(piece, phase, d):
        block = piece(held_by(d))
        remote(
            block, block, tok_send.at[phase, d], tok_recv.at[phase, d], along_x[d]
        ).wait_recv()
        go(x_pass_copy(piece, phase, d))

    def x_from_sibling(piece, phase, d):
        block = piece(held_by(d, True))
        n = 0 if d == 0 else 3 + d
        remote(block, block, tok_send.at[phase, n], tok_recv.at[phase, n], sibling).wait_recv()

    for d in (1, 3, 2, 0):
        go(x_copy(token_piece, 0, d))

    for n in (1, 2):
        mine[n].wait()
    ring_stage(FRONT, 1)

    def pass_on_qkv(dz):
        qkv_over_z(dz, True).wait_recv()
        for copy in qkv_over_y(dz):
            go(copy)

    for dz in (1, 7, 2, 6):
        pass_on_qkv(dz)
    shard_arrived(OUT)
    for dz in (1, 7, 2, 6, 3, 5, 4):
        go(out_over_z(dz))
    for dz in (3, 5, 4):
        pass_on_qkv(dz)
    for part in (DOWN, REST):
        shard_arrived(part)
        ring_stage(part, 1)

    length = lengths[0]

    def key_bias(n, carry):
        at = pl.multiple_of(n * PAIR, PAIR)
        row = rows_of((PAIR, HQ)) + at
        slot = jnp.where(row < CYCLE - HEAD, row + HEAD, row - (CYCLE - HEAD))
        lag = length - 1 - SINK - slot
        turns = (
            jnp.where(lag >= CYCLE, 1, 0)
            + jnp.where(lag >= 2 * CYCLE, 1, 0)
            + jnp.where(lag >= 3 * CYCLE, 1, 0)
        )
        held = SINK + slot + CYCLE * turns
        old = (lag >= 0) & (held >= length - WINDOW) & (row < OLD + 12)
        seen = old | ((row >= OLD + 12) & (row < NEW_AT + TOK))
        keys[pl.ds(at, PAIR), HQ : 2 * HQ] = jnp.where(seen, 0.0, AWAY).astype(BF16)
        values[pl.ds(at, PAIR), HQ : 2 * HQ] = jnp.ones((PAIR, HQ), BF16)
        return carry

    lax.fori_loop(0, KEYS // PAIR, key_bias, 0)
    spare = KEYS - NEW_AT - TOK
    for load in loads:
        load.wait()
    tile_row = rows_of((16, HQ))
    for kind, store in ((0, keys), (1, values)):
        store[NEW_AT + TOK :, 0:HQ] = jnp.zeros((spare, HQ), BF16)
        tile = store[OLD:NEW_AT, 0:HQ].astype(F32)
        sink_rows = sinks[0, kind].astype(F32)
        for r in range(SINK):
            tile = jnp.where(tile_row == 12 + r, sink_rows[r : r + 1], tile)
        store[OLD:NEW_AT, 0:HQ] = tile.astype(BF16)

    for d in (1, 3, 2):
        x_pass_on(token_piece, 0, d)

    def assemble(p, take, put):
        zz, pair = p // 2, lax.rem(p, 2)
        low, high = take(zz, 2 * pair), take(zz, 2 * pair + 1)
        put(
            pl.ds(pl.multiple_of(p * 2 * SHARD, 16), 2 * SHARD),
            jnp.concatenate([low.astype(F32), high.astype(F32)], axis=0).astype(BF16),
        )

    def put_out(rows, value):
        g_out[gx, rows, :] = value

    def assemble_out(p, carry):
        assemble(p, lambda zz, yy: l_out[zz, yy], put_out)
        return carry

    for dz in (1, 7, 2, 6, 3, 5, 4):
        out_over_z(dz, True).wait_recv()
    lax.fori_loop(0, D // (2 * SHARD), assemble_out, 0)
    for d in (2, 1, 3, 0):
        go(x_copy(out_piece, 1, d))
    ring_stage(FRONT, 2)
    for n in range(ZC):
        for d in (1, 2, 3):
            piece = l_qkv.at[lax.rem(z + ZC - n, ZC), from_y(d)]
            remote(
                piece, piece, qkv_send.at[d, n], qkv_recv.at[d, n], along_y[d]
            ).wait_recv()
    for n in (0, 1, 7):
        for copy in front_over_y(n):
            go(copy)

    def assemble_qkv(p, carry):
        for n in range(3):

            def put(rows, value, n=n):
                g_qkv[rows, n * HQ : (n + 1) * HQ] = value

            assemble(p, lambda zz, yy, n=n: l_qkv[zz, yy, n], put)
        return carry

    lax.fori_loop(0, D // (2 * SHARD), assemble_qkv, 0)
    for d in (0, 1, 2, 3):
        x_from_sibling(token_piece, 0, d)

    low_head = lanes((PAIR, HQ)) < 64

    def head_unit(v):
        squares = v * v
        low = jnp.sum(jnp.where(low_head, squares, 0.0), axis=-1, keepdims=True)
        high = jnp.sum(jnp.where(low_head, 0.0, squares), axis=-1, keepdims=True)
        return v * jnp.where(low_head, lax.rsqrt(low + 1e-06), lax.rsqrt(high + 1e-06))

    def project(n, carry):
        at = pl.multiple_of(n * PAIR, PAIR)
        qkv = dot(tokens[pl.ds(at, PAIR), :], g_qkv[...])
        scale = s_qk[...]
        q = (head_unit(qkv[:, 0:HQ]) * scale).astype(BF16)
        queries[pl.ds(at, PAIR), :] = (q.astype(F32) * 8.0).astype(BF16)
        k = (head_unit(qkv[:, HQ : 2 * HQ]) * scale).astype(BF16)
        v = qkv[:, 2 * HQ :].astype(BF16)
        to = pl.ds(pl.multiple_of(NEW_AT + at, 16), PAIR)
        keys[to, 0:HQ] = k
        values[to, 0:HQ] = v
        fresh[0, 0, pl.ds(at, PAIR), :] = k
        fresh[0, 1, pl.ds(at, PAIR), :] = v
        return carry

    lax.fori_loop(0, TOK // PAIR, project, 0)
    ring_stage(DOWN, 2)
    ring_stage(REST, 2)
    ring_stage(FRONT, 3)
    for n in (2, 6):
        for copy in front_over_y(n):
            go(copy)

    def own_half(ref):
        return ref[pl.ds(pl.multiple_of(c * OWN, OWN), OWN), :]

    def other_half(ref):
        return ref[pl.ds(pl.multiple_of((1 - c) * OWN, OWN), OWN), :]

    def sib_copy(k):
        return remote(
            to_sib.at[k],
            from_sib.at[k],
            sib_send.at[k],
            sib_recv.at[k],
            sibling,
        )

    def owner_copy(k, d):
        to = (lax.rem(x + d, XC) * 2 + c, gy)
        return remote(
            to_owner.at[k],
            from_peer.at[k],
            sum_send.at[k],
            sum_recv.at[k],
            to,
        )

    def give_halves(k):
        kept[k] = own_half(partial)
        to_sib[k] = other_half(partial).astype(BF16)
        sib_copy(k).start()

    def chip_sum(k):
        sib_copy(k).wait_recv()
        return kept[k] + from_sib[k].astype(F32)

    def send_sum(k, d):
        to_owner[k] = chip_sum(k).astype(BF16)
        owner_copy(k, d).start()

    query_row = jnp.where(
        rows_of((2 * PAIR, CHUNK)) >= PAIR, rows_of((2 * PAIR, CHUNK)) - PAIR, rows_of((2 * PAIR, CHUNK))
    )
    key_col = lanes((2 * PAIR, CHUNK))

    def left_side(k):
        q = queries[k * PAIR : (k + 1) * PAIR, :]
        zero = jnp.zeros_like(q)
        both = jnp.concatenate([jnp.where(low_head, q, zero), jnp.where(low_head, zero, q)], axis=0)
        return jnp.concatenate([both, jnp.ones((2 * PAIR, HQ), BF16)], axis=1)

    def score(k, n, lhs, top):
        s = dot_nt(lhs, keys[k * PAIR + n * CHUNK : k * PAIR + (n + 1) * CHUNK, :])
        if n == 0:
            s = jnp.where(key_col >= query_row + FIRST, s, AWAY)
        if n == CHUNKS - 1:
            s = jnp.where(key_col + n * CHUNK <= query_row + NEW_AT, s, AWAY)
        (even_scores, odd_scores)[k % 2][:, n * CHUNK : (n + 1) * CHUNK] = s
        part = jnp.maximum(s[:, 0:HQ], s[:, HQ:])
        return part if top is None else jnp.maximum(top, part)

    def weigh(k, n, highest, weighted):
        s = (even_scores, odd_scores)[k % 2][:, n * CHUNK : (n + 1) * CHUNK]
        w = jnp.exp(s - highest).astype(BF16)
        part = dot(w, values[k * PAIR + n * CHUNK : k * PAIR + (n + 1) * CHUNK, :])
        return part if weighted is None else weighted + part

    def attend():
        highest = None
        for k in range(5):
            if k == 2:
                ring_stage(FRONT, 4)
                for n in (3, 5):
                    for copy in front_over_y(n):
                        go(copy)
            if k == 4:
                ring_stage(DOWN, 3)
                ring_stage(REST, 3)
            top, weighted = None, None
            lhs = left_side(k) if k < 4 else None
            for n in range(CHUNKS):
                if k > 0:
                    weighted = weigh(k - 1, n, highest, weighted)
                if k < 4:
                    top = score(k, n, lhs, top)
            if k > 0:
                mean = weighted[:, 0:HQ] / weighted[:, HQ:]
                attended[gx, (k - 1) * PAIR : k * PAIR, :] = jnp.where(
                    low_head, mean[0:PAIR], mean[PAIR:]
                ).astype(BF16)
                for d in range(XC):
                    go(x_copy(attended_piece(k - 1), 1 + k, d))
            if k < 4:
                highest = jnp.max(top, axis=-1, keepdims=True)

    def finish(part):
        for way in (0, 1):
            if last_step(part, way) == 4:
                ring_copy(part, way, 4, True).wait_recv()

    attend()
    finish(FRONT)
    for copy in front_over_y(4):
        go(copy)
    for d in (1, 3, 2):
        x_pass_on(out_piece, 1, d)
    for n in range(3):
        for d in (1, 3, 2):
            x_pass_on(attended_piece(n), 2 + n, d)

    def wide_row(ref, count):
        return jnp.concatenate([ref[n : n + 1, :] for n in range(count)], axis=1)

    alpha_a = wide_row(alpha_attn, D // HQ)

    def update(k, carry):
        rows = slice(k * PAIR, (k + 1) * PAIR)
        heads = jnp.concatenate([attended[g, rows, :] for g in range(2 * XC)], axis=1)
        out = jnp.concatenate([g_out[g] for g in range(2 * XC)], axis=1)
        mixed = dot_nt(heads, out)
        residual = tokens[rows, :].astype(F32)
        after[rows, :] = rms_unit(residual + alpha_a * (rms_unit(mixed) - residual)).astype(BF16)
        return carry

    for d in range(XC):
        x_from_sibling(out_piece, 1, d)
    for n in range(4):
        for d in range(XC):
            x_from_sibling(attended_piece(n), 2 + n, d)
        update(n, 0)
        if n == 0:
            for d in (1, 3, 2):
                x_pass_on(attended_piece(3), 5, d)
    ring_stage(DOWN, 4)
    ring_stage(REST, 4)

    for n in range(ZC):
        for d in (1, 2, 3):
            piece = l_front.at[lax.rem(z + ZC - n, ZC), from_y(d)]
            remote(
                piece, piece, quarter_send.at[n, d - 1], quarter_recv.at[n, d - 1], along_y[d]
            ).wait_recv()

    def gate_block(b):
        at = b * HQ
        if at < GATE_FRONT:
            return lambda zz, yy: l_front[zz, yy, :, FF + at : FF + at + HQ]
        at -= GATE_FRONT
        return lambda zz, yy: l_rest[zz, yy, :, at : at + HQ]

    def assemble_ff(p, carry):
        for b in range(FF // HQ):

            def put_up(rows, value, b=b):
                g_ff[b, rows, 0:HQ] = value

            def put_gate(rows, value, b=b):
                g_ff[b, rows, HQ : 2 * HQ] = value

            assemble(p, lambda zz, yy, b=b: l_front[zz, yy, :, b * HQ : (b + 1) * HQ], put_up)
            assemble(p, gate_block(b), put_gate)

        def put_down(rows, value):
            g_down[rows, :] = value

        assemble(p, lambda zz, yy: l_down[zz, yy], put_down)
        return carry

    finish(DOWN)
    finish(REST)
    lax.fori_loop(0, D // (2 * SHARD), assemble_ff, 0)

    s_up_row = wide_row(s_up, FF // HQ)
    s_gate_row = wide_row(s_gate, FF // HQ)

    def far_first(k):
        return jnp.where(k == 0, 2, jnp.where(k == 1, 1, jnp.where(k == 2, 3, 0)))

    def feed(k):
        block = lax.rem(x + far_first(k), XC)
        rows = after[pl.ds(pl.multiple_of(block * PAIR, PAIR), PAIR), :]
        acts = []
        for b in range(5):
            both = dot(rows, g_ff[b])
            cols = slice(b * HQ, b * HQ + HQ)
            up = both[:, 0:HQ] * s_up_row[:, cols]
            gate = both[:, HQ:] * s_gate_row[:, cols]
            acts.append((up * (gate / (1.0 + jnp.exp(-gate)))).astype(BF16))
        active = jnp.concatenate(acts, axis=1)
        partial[...] = dot_nt(active, g_down[...])
        give_halves(k)

    def feed_step(k, carry):
        feed(k)

        @pl.when(k >= 1)
        def _():
            send_sum(k - 1, far_first(k - 1))

        return carry

    lax.fori_loop(0, 4, feed_step, 0)
    lowered = chip_sum(3)
    for k, d in ((0, 2), (1, 1), (2, 3)):
        owner_copy(k, d).wait_recv()
        lowered = lowered + from_peer[k].astype(F32)
    wide = after[block_of(gx), :].astype(F32)
    alpha_m = wide_row(alpha_mlp, D // HQ)
    result[0] = rms_unit(wide + alpha_m * (rms_unit(lowered) - wide)).astype(BF16)

    for copy in sent:
        copy.wait_send()
    for k in range(4):
        sib_copy(k).wait_send()
    for k, d in ((0, 2), (1, 1), (2, 3)):
        owner_copy(k, d).wait_send()


SPAN = TOK + 16


BANDS = 4


def append_kernel(
    lengths, cached, fresh, hidden, new_hidden, new_cycle, cycle, new_rows, own, sem
):
    start = jnp.clip(lax.rem(lengths[0] - SINK, CYCLE), 0, CYCLE - SPAN)
    base = pl.multiple_of(start // 16 * 16, 16)
    shift = start - base
    bands = [(n, b, pl.ds(b * (CYCLE // BANDS), CYCLE // BANDS)) for n in (0, 1) for b in range(BANDS)]
    loads = [pltpu.make_async_copy(cached.at[0, n, r], cycle.at[n, r], sem.at[0, n, b]) for n, b, r in bands]
    stores = [pltpu.make_async_copy(cycle.at[n, r], new_cycle.at[0, n, r], sem.at[1, n, b]) for n, b, r in bands]
    rows_in = pltpu.make_async_copy(fresh.at[0], new_rows, sem.at[2, 0, 0])
    own_in = pltpu.make_async_copy(hidden.at[0], own, sem.at[2, 0, 1])
    own_out = pltpu.make_async_copy(own, new_hidden.at[0], sem.at[2, 0, 2])
    for load in (rows_in, own_in, *loads):
        load.start()
    row = rows_of((SPAN, HQ))
    here = (row >= shift) & (row < shift + TOK)
    rows_in.wait()
    for n in (0, 1):
        rows = jnp.concatenate([new_rows[n].astype(F32), jnp.zeros((16, HQ), F32)], axis=0)
        rows = pltpu.roll(rows, shift, 0)
        if n == 0:
            own_in.wait()
            own_out.start()
        for load in loads[n * BANDS : (n + 1) * BANDS]:
            load.wait()
        window = cycle.at[n, pl.ds(base, SPAN)]
        window[...] = jnp.where(here, rows, window[...].astype(F32)).astype(BF16)
        for store in stores[n * BANDS : (n + 1) * BANDS]:
            store.start()
    for copy in (*stores, own_out):
        copy.wait()


def per_device(
    hidden,
    lengths,
    sink_kv,
    kv_cycle,
    w_qkv,
    s_qk,
    w_out,
    alpha_attn,
    w_up,
    w_gate,
    s_up,
    s_gate,
    w_down,
    alpha_mlp,
):
    vmem = pl.BlockSpec(memory_space=pltpu.VMEM)
    anywhere = pl.BlockSpec(memory_space=pl.ANY)
    dma = pltpu.SemaphoreType.DMA
    result, fresh = pl.pallas_call(
        layer_kernel,
        out_shape=(
            jax.ShapeDtypeStruct((1, OWN, D), BF16),
            jax.ShapeDtypeStruct((1, 2, TOK, HQ), BF16),
        ),
        in_specs=[
            pl.BlockSpec(memory_space=pltpu.SMEM),
            anywhere,
            vmem,
            anywhere,
            anywhere,
            vmem,
            anywhere,
            vmem,
            anywhere,
            anywhere,
            vmem,
            vmem,
            anywhere,
            vmem,
        ],
        out_specs=(vmem, vmem),
        scratch_shapes=[
            pltpu.VMEM((ZC, YC, 3, SHARD, HQ), BF16),
            pltpu.VMEM((ZC, YC, SHARD, HQ), BF16),
            pltpu.VMEM((ZC, YC, SHARD, FF), BF16),
            pltpu.VMEM((ZC, YC, SHARD, GATE_REST), BF16),
            pltpu.VMEM((ZC, YC, SHARD, FF + GATE_FRONT), BF16),
            pltpu.VMEM((D, 3 * HQ), BF16),
            pltpu.VMEM((2 * XC, D, HQ), BF16),
            pltpu.VMEM((5, D, 2 * HQ), BF16),
            pltpu.VMEM((D, FF), BF16),
            pltpu.VMEM((TOK, D), BF16),
            pltpu.VMEM((KEYS, 2 * HQ), BF16),
            pltpu.VMEM((KEYS, 2 * HQ), BF16),
            pltpu.VMEM((TOK, HQ), BF16),
            pltpu.VMEM((2 * PAIR, CHUNK * CHUNKS), F32),
            pltpu.VMEM((2 * PAIR, CHUNK * CHUNKS), F32),
            pltpu.VMEM((2 * XC, TOK, HQ), BF16),
            pltpu.VMEM((PAIR, D), F32),
            pltpu.VMEM((4, OWN, D), F32),
            pltpu.VMEM((4, OWN, D), BF16),
            pltpu.VMEM((4, OWN, D), BF16),
            pltpu.VMEM((4, OWN, D), BF16),
            pltpu.VMEM((4, OWN, D), BF16),
            pltpu.VMEM((TOK, D), BF16),
            dma((11,)),
            dma((6, 7)),
            dma((6, 7)),
            dma((4, ZC)),
            dma((4, ZC)),
            dma((ZC,)),
            dma((ZC,)),
            dma((3, 3)),
            dma((3, 3)),
            dma((3, 2, 4)),
            dma((3, 2, 4)),
            dma((ZC, 3)),
            dma((ZC, 3)),
            dma((4,)),
            dma((4,)),
            dma((4,)),
            dma((4,)),
        ],
        compiler_params=pltpu.CompilerParams(
            collective_id=0, has_side_effects=True, vmem_limit_bytes=56 * 2**20
        ),
    )(
        lengths,
        hidden,
        sink_kv,
        kv_cycle,
        w_qkv.transpose(1, 0, 2),
        s_qk.reshape(1, HQ),
        w_out.T,
        alpha_attn.reshape(D // HQ, HQ),
        w_up,
        w_gate,
        s_up.reshape(FF // HQ, HQ),
        s_gate.reshape(FF // HQ, HQ),
        w_down.T,
        alpha_mlp.reshape(D // HQ, HQ),
    )
    return pl.pallas_call(
        append_kernel,
        out_shape=(
            jax.ShapeDtypeStruct((1, OWN, D), BF16),
            jax.ShapeDtypeStruct(kv_cycle.shape, BF16),
        ),
        in_specs=[pl.BlockSpec(memory_space=pltpu.SMEM), anywhere, anywhere, anywhere],
        out_specs=(anywhere, anywhere),
        scratch_shapes=[
            pltpu.VMEM((2, CYCLE, HQ), BF16),
            pltpu.VMEM((2, TOK, HQ), BF16),
            pltpu.VMEM((OWN, D), BF16),
            dma((3, 2, BANDS)),
        ],
        compiler_params=pltpu.CompilerParams(vmem_limit_bytes=56 * 2**20),
    )(lengths, kv_cycle, fresh, result)


def solution(mesh):
    return jax.shard_map(
        per_device,
        mesh=mesh,
        in_specs=(
            P("gy", "gx", None),
            P("gy"),
            P("gy", None, None, "gx"),
            P("gy", None, None, "gx"),
            P("gy", None, "gx"),
            P("gx"),
            P("gx", "gy"),
            P(),
            P("gy", "gx"),
            P("gy", "gx"),
            P("gx"),
            P("gx"),
            P("gx", "gy"),
            P(),
        ),
        out_specs=(P("gy", "gx", None), P("gy", None, None, "gx")),
        check_vma=False,
    )
```

```python
import functools

import jax
import jax.numpy as jnp
from jax import lax
from jax.experimental import pallas as pl
from jax.experimental.pallas import tpu as pltpu
from jax.sharding import PartitionSpec as P

MESH = pl.DeviceIdType.MESH
BF16 = jnp.bfloat16
F32 = jnp.float32

XC, YC, ZC = 4, 4, 8
D = 1280
HQ = 128
FF = 640
TOK = 512
OWN = 64
PAIR = 128
SHARD = 40
PLANE = SHARD * YC
SINK = 4
WINDOW = 4096
CYCLE = 4608
LONG = 16384
HEAD = 3056
TAIL = 2544
OLD = CYCLE - HEAD + TAIL
NEW_AT = OLD + 16
CHUNK = 256
CHUNKS = 17
KEYS = 3 * PAIR + CHUNK * CHUNKS
FIRST = 13
AWAY = -1e30
DOWN, REST, FRONT = 0, 1, 2
OUT = 2
GATE_FRONT = 256
GATE_REST = FF - GATE_FRONT
RIGHT_LAST = (DOWN,)


def dot(a, b):
    return jnp.dot(a, b, preferred_element_type=F32)


def dot_nt(a, b):
    return lax.dot_general(a, b, (((1,), (1,)), ((), ())), preferred_element_type=F32)


def rms_unit(values):
    return values * lax.rsqrt(jnp.mean(values * values, axis=-1, keepdims=True) + 1e-06)


def lanes(shape):
    return lax.broadcasted_iota(jnp.int32, shape, len(shape) - 1)


def rows_of(shape):
    return lax.broadcasted_iota(jnp.int32, shape, len(shape) - 2)


def layer_kernel(
    lengths,
    hidden,
    sinks,
    cached,
    w_qkv,
    s_qk,
    w_out,
    alpha_attn,
    w_up,
    w_gate,
    s_up,
    s_gate,
    w_down,
    alpha_mlp,
    result,
    fresh,
    l_qkv,
    l_out,
    l_down,
    l_rest,
    l_front,
    g_qkv,
    g_out,
    g_ff,
    g_down,
    tokens,
    keys,
    values,
    queries,
    even_scores,
    odd_scores,
    attended,
    partial,
    kept,
    to_sib,
    from_sib,
    to_owner,
    from_peer,
    after,
    local_sem,
    tok_send,
    tok_recv,
    qkv_send,
    qkv_recv,
    out_send,
    out_recv,
    shard_send,
    shard_recv,
    ring_send,
    ring_recv,
    quarter_send,
    quarter_recv,
    sib_send,
    sib_recv,
    sum_send,
    sum_recv,
):
    gx = lax.axis_index("gx")
    gy = lax.axis_index("gy")
    x, c = gx // 2, lax.rem(gx, 2)
    z, y = gy // YC, lax.rem(gy, YC)

    def device(dx=0, other=False, dz=0, dy=0):
        core = 1 - c if other else c
        return (
            lax.rem(x + dx, XC) * 2 + core,
            lax.rem(z + dz, ZC) * YC + lax.rem(y + dy, YC),
        )

    sibling = device(other=True)
    along_x = {d: device(dx=d) for d in (1, 2, 3)}
    along_y = {d: device(dy=d) for d in (1, 2, 3)}
    right, left = device(dz=1), device(dz=ZC - 1)
    along_z = [device(dz=d) for d in range(1, ZC)]
    everyone = [sibling, *along_x.values(), *along_y.values(), *along_z]
    gate_sem = pltpu.get_barrier_semaphore()
    for peer in everyone:
        pl.semaphore_signal(gate_sem, inc=1, device_id=peer, device_id_type=MESH)

    sent = []

    def remote(src, dst, send, recv, to):
        return pltpu.make_async_remote_copy(
            src_ref=src, dst_ref=dst, send_sem=send, recv_sem=recv, device_id=to, device_id_type=MESH
        )

    def go(copy):
        copy.start()
        sent.append(copy)

    def block_of(g):
        return pl.ds(pl.multiple_of(g * OWN, OWN), OWN)

    own_in = pltpu.make_async_copy(hidden.at[0], tokens.at[block_of(gx)], local_sem.at[0])
    own_in.start()
    loads = []
    for kind, store in ((0, keys), (1, values)):
        for n, (src, at, count) in enumerate(
            ((HEAD, 0, CYCLE - HEAD), (0, CYCLE - HEAD, TAIL + 16))
        ):
            loads.append(
                pltpu.make_async_copy(
                    cached.at[0, kind, pl.ds(src, count)],
                    store.at[pl.ds(at, count), pl.ds(0, HQ)],
                    local_sem.at[1 + 2 * kind + n],
                )
            )
    for load in loads:
        load.start()

    mine = [
        (w_qkv, l_qkv.at[z, y]),
        (w_up, l_front.at[z, y, :, pl.ds(0, FF)]),
        (w_gate.at[:, pl.ds(0, GATE_FRONT)], l_front.at[z, y, :, pl.ds(FF, GATE_FRONT)]),
        (w_gate.at[:, pl.ds(GATE_FRONT, GATE_REST)], l_rest.at[z, y, :, pl.ds(0, GATE_REST)]),
        (w_down, l_down.at[z, y]),
        (w_out, l_out.at[z, y]),
    ]
    mine = [pltpu.make_async_copy(a, b, local_sem.at[5 + n]) for n, (a, b) in enumerate(mine)]
    for copy in mine:
        copy.start()

    def over_y(piece, sends, recvs):
        return [remote(piece, piece, sends(d - 1), recvs(d - 1), along_y[d]) for d in (1, 2, 3)]

    def qkv_over_z(dz, arriving=False):
        zz = lax.rem(z + ZC - dz, ZC) if arriving else z
        piece = l_qkv.at[zz, y]
        return remote(piece, piece, qkv_send.at[0, dz], qkv_recv.at[0, dz], device(dz=dz))

    def qkv_over_y(dz):
        piece = l_qkv.at[lax.rem(z + ZC - dz, ZC), y]
        return over_y(piece, lambda n: qkv_send.at[1 + n, dz], lambda n: qkv_recv.at[1 + n, dz])

    def out_over_z(dz, arriving=False):
        piece = l_out.at[lax.rem(z + ZC - dz, ZC) if arriving else z]
        return remote(piece, piece, out_send.at[dz], out_recv.at[dz], device(dz=dz))

    def from_y(d):
        return lax.rem(y + YC - d, YC)

    def shard_over_y(part):
        piece = (l_down, l_rest, l_out)[part].at[z, y]
        return over_y(piece, lambda n: shard_send.at[part, n], lambda n: shard_recv.at[part, n])

    def shard_arrived(part):
        for d in (1, 2, 3):
            piece = (l_down, l_rest, l_out)[part].at[z, from_y(d)]
            remote(
                piece, piece, shard_send.at[part, d - 1], shard_recv.at[part, d - 1], along_y[d]
            ).wait_recv()

    def last_step(part, way):
        return 4 if (part in RIGHT_LAST) == (way == 0) else 3

    def ring_copy(part, way, step, arriving):
        back = step if arriving else step - 1
        zz = lax.rem(z + ZC - back, ZC) if way == 0 else lax.rem(z + back, ZC)
        piece = (l_down.at[zz], l_rest.at[zz], l_front.at[zz, y])[part]
        return remote(
            piece,
            piece,
            ring_send.at[part, way, step - 1],
            ring_recv.at[part, way, step - 1],
            right if way == 0 else left,
        )

    def front_over_y(n):
        piece = l_front.at[lax.rem(z + ZC - n, ZC), y]
        return over_y(piece, lambda m: quarter_send.at[n, m], lambda m: quarter_recv.at[n, m])

    def ring_stage(part, step):
        for way in (0, 1):
            if 1 <= step - 1 <= last_step(part, way):
                ring_copy(part, way, step - 1, True).wait_recv()
            if step <= last_step(part, way):
                go(ring_copy(part, way, step, False))

    pl.semaphore_wait(gate_sem, len(everyone))
    mine[0].wait()
    for dz in (1, 7, 2, 6, 3, 5, 4):
        go(qkv_over_z(dz))
    mine[5].wait()
    for copy in (*shard_over_y(OUT), *qkv_over_y(0)):
        go(copy)
    for n in (3, 4):
        mine[n].wait()
    for part in (DOWN, REST):
        for copy in shard_over_y(part):
            go(copy)

    own_in.wait()

    def held_by(d, other=False):
        core = 1 - c if other else c
        return lax.rem(x + XC - d, XC) * 2 + core

    def token_piece(g):
        return tokens.at[block_of(g)]

    def out_piece(g):
        return g_out.at[g]

    def attended_piece(n):
        return lambda g: attended.at[g, pl.ds(pl.multiple_of(n * PAIR, PAIR), PAIR)]

    def x_copy(piece, phase, d):
        to = sibling if d == 0 else along_x[d]
        return remote(piece(gx), piece(gx), tok_send.at[phase, d], tok_recv.at[phase, d], to)

    def x_pass_copy(piece, phase, d):
        block = piece(held_by(d))
        return remote(block, block, tok_send.at[phase, 3 + d], tok_recv.at[phase, 3 + d], sibling)

    def x_pass_on(piece, phase, d):
        block = piece(held_by(d))
        remote(
            block, block, tok_send.at[phase, d], tok_recv.at[phase, d], along_x[d]
        ).wait_recv()
        go(x_pass_copy(piece, phase, d))

    def x_from_sibling(piece, phase, d):
        block = piece(held_by(d, True))
        n = 0 if d == 0 else 3 + d
        remote(block, block, tok_send.at[phase, n], tok_recv.at[phase, n], sibling).wait_recv()

    for d in (1, 3, 2, 0):
        go(x_copy(token_piece, 0, d))

    for n in (1, 2):
        mine[n].wait()
    ring_stage(FRONT, 1)

    def pass_on_qkv(dz):
        qkv_over_z(dz, True).wait_recv()
        for copy in qkv_over_y(dz):
            go(copy)

    for dz in (1, 7, 2, 6):
        pass_on_qkv(dz)
    shard_arrived(OUT)
    for dz in (1, 7, 2, 6, 3, 5, 4):
        go(out_over_z(dz))
    for dz in (3, 5, 4):
        pass_on_qkv(dz)
    for part in (DOWN, REST):
        shard_arrived(part)
        ring_stage(part, 1)

    length = lengths[0]

    def key_bias(n, carry):
        at = pl.multiple_of(n * PAIR, PAIR)
        row = rows_of((PAIR, HQ)) + at
        slot = jnp.where(row < CYCLE - HEAD, row + HEAD, row - (CYCLE - HEAD))
        lag = length - 1 - SINK - slot
        turns = (
            jnp.where(lag >= CYCLE, 1, 0)
            + jnp.where(lag >= 2 * CYCLE, 1, 0)
            + jnp.where(lag >= 3 * CYCLE, 1, 0)
        )
        held = SINK + slot + CYCLE * turns
        old = (lag >= 0) & (held >= length - WINDOW) & (row < OLD + 12)
        seen = old | ((row >= OLD + 12) & (row < NEW_AT + TOK))
        keys[pl.ds(at, PAIR), HQ : 2 * HQ] = jnp.where(seen, 0.0, AWAY).astype(BF16)
        values[pl.ds(at, PAIR), HQ : 2 * HQ] = jnp.ones((PAIR, HQ), BF16)
        return carry

    lax.fori_loop(0, KEYS // PAIR, key_bias, 0)
    spare = KEYS - NEW_AT - TOK
    for load in loads:
        load.wait()
    tile_row = rows_of((16, HQ))
    for kind, store in ((0, keys), (1, values)):
        store[NEW_AT + TOK :, 0:HQ] = jnp.zeros((spare, HQ), BF16)
        tile = store[OLD:NEW_AT, 0:HQ].astype(F32)
        sink_rows = sinks[0, kind].astype(F32)
        for r in range(SINK):
            tile = jnp.where(tile_row == 12 + r, sink_rows[r : r + 1], tile)
        store[OLD:NEW_AT, 0:HQ] = tile.astype(BF16)

    for d in (1, 3, 2):
        x_pass_on(token_piece, 0, d)

    def assemble(p, take, put):
        zz, pair = p // 2, lax.rem(p, 2)
        low, high = take(zz, 2 * pair), take(zz, 2 * pair + 1)
        put(
            pl.ds(pl.multiple_of(p * 2 * SHARD, 16), 2 * SHARD),
            jnp.concatenate([low.astype(F32), high.astype(F32)], axis=0).astype(BF16),
        )

    def put_out(rows, value):
        g_out[gx, rows, :] = value

    def assemble_out(p, carry):
        assemble(p, lambda zz, yy: l_out[zz, yy], put_out)
        return carry

    for dz in (1, 7, 2, 6, 3, 5, 4):
        out_over_z(dz, True).wait_recv()
    lax.fori_loop(0, D // (2 * SHARD), assemble_out, 0)
    for d in (2, 1, 3, 0):
        go(x_copy(out_piece, 1, d))
    ring_stage(FRONT, 2)
    for n in range(ZC):
        for d in (1, 2, 3):
            piece = l_qkv.at[lax.rem(z + ZC - n, ZC), from_y(d)]
            remote(
                piece, piece, qkv_send.at[d, n], qkv_recv.at[d, n], along_y[d]
            ).wait_recv()
    for n in (0, 1, 7):
        for copy in front_over_y(n):
            go(copy)

    def assemble_qkv(p, carry):
        for n in range(3):

            def put(rows, value, n=n):
                g_qkv[rows, n * HQ : (n + 1) * HQ] = value

            assemble(p, lambda zz, yy, n=n: l_qkv[zz, yy, n], put)
        return carry

    lax.fori_loop(0, D // (2 * SHARD), assemble_qkv, 0)
    for d in (0, 1, 2, 3):
        x_from_sibling(token_piece, 0, d)

    low_head = lanes((PAIR, HQ)) < 64

    def head_unit(v):
        squares = v * v
        low = jnp.sum(jnp.where(low_head, squares, 0.0), axis=-1, keepdims=True)
        high = jnp.sum(jnp.where(low_head, 0.0, squares), axis=-1, keepdims=True)
        return v * jnp.where(low_head, lax.rsqrt(low + 1e-06), lax.rsqrt(high + 1e-06))

    def project(n, carry):
        at = pl.multiple_of(n * PAIR, PAIR)
        qkv = dot(tokens[pl.ds(at, PAIR), :], g_qkv[...])
        scale = s_qk[...]
        q = (head_unit(qkv[:, 0:HQ]) * scale).astype(BF16)
        queries[pl.ds(at, PAIR), :] = (q.astype(F32) * 8.0).astype(BF16)
        k = (head_unit(qkv[:, HQ : 2 * HQ]) * scale).astype(BF16)
        v = qkv[:, 2 * HQ :].astype(BF16)
        to = pl.ds(pl.multiple_of(NEW_AT + at, 16), PAIR)
        keys[to, 0:HQ] = k
        values[to, 0:HQ] = v
        fresh[0, 0, pl.ds(at, PAIR), :] = k
        fresh[0, 1, pl.ds(at, PAIR), :] = v
        return carry

    lax.fori_loop(0, TOK // PAIR, project, 0)
    ring_stage(DOWN, 2)
    ring_stage(REST, 2)
    ring_stage(FRONT, 3)
    for n in (2, 6):
        for copy in front_over_y(n):
            go(copy)

    def own_half(ref):
        return ref[pl.ds(pl.multiple_of(c * OWN, OWN), OWN), :]

    def other_half(ref):
        return ref[pl.ds(pl.multiple_of((1 - c) * OWN, OWN), OWN), :]

    def sib_copy(k):
        return remote(
            to_sib.at[k],
            from_sib.at[k],
            sib_send.at[k],
            sib_recv.at[k],
            sibling,
        )

    def owner_copy(k, d):
        to = (lax.rem(x + d, XC) * 2 + c, gy)
        return remote(
            to_owner.at[k],
            from_peer.at[k],
            sum_send.at[k],
            sum_recv.at[k],
            to,
        )

    def give_halves(k):
        kept[k] = own_half(partial)
        to_sib[k] = other_half(partial).astype(BF16)
        sib_copy(k).start()

    def chip_sum(k):
        sib_copy(k).wait_recv()
        return kept[k] + from_sib[k].astype(F32)

    def send_sum(k, d):
        to_owner[k] = chip_sum(k).astype(BF16)
        owner_copy(k, d).start()

    query_row = jnp.where(
        rows_of((2 * PAIR, CHUNK)) >= PAIR, rows_of((2 * PAIR, CHUNK)) - PAIR, rows_of((2 * PAIR, CHUNK))
    )
    key_col = lanes((2 * PAIR, CHUNK))

    def left_side(k):
        q = queries[k * PAIR : (k + 1) * PAIR, :]
        zero = jnp.zeros_like(q)
        both = jnp.concatenate([jnp.where(low_head, q, zero), jnp.where(low_head, zero, q)], axis=0)
        return jnp.concatenate([both, jnp.ones((2 * PAIR, HQ), BF16)], axis=1)

    def score(k, n, lhs, top):
        s = dot_nt(lhs, keys[k * PAIR + n * CHUNK : k * PAIR + (n + 1) * CHUNK, :])
        if n == 0:
            s = jnp.where(key_col >= query_row + FIRST, s, AWAY)
        if n == CHUNKS - 1:
            s = jnp.where(key_col + n * CHUNK <= query_row + NEW_AT, s, AWAY)
        (even_scores, odd_scores)[k % 2][:, n * CHUNK : (n + 1) * CHUNK] = s
        part = jnp.maximum(s[:, 0:HQ], s[:, HQ:])
        return part if top is None else jnp.maximum(top, part)

    def weigh(k, n, highest, weighted):
        s = (even_scores, odd_scores)[k % 2][:, n * CHUNK : (n + 1) * CHUNK]
        w = jnp.exp(s - highest).astype(BF16)
        part = dot(w, values[k * PAIR + n * CHUNK : k * PAIR + (n + 1) * CHUNK, :])
        return part if weighted is None else weighted + part

    def attend():
        highest = None
        for k in range(5):
            if k == 2:
                ring_stage(FRONT, 4)
                for n in (3, 5):
                    for copy in front_over_y(n):
                        go(copy)
            if k == 4:
                ring_stage(DOWN, 3)
                ring_stage(REST, 3)
                for d in (1, 3, 2):
                    x_pass_on(out_piece, 1, d)
            top, weighted = None, None
            lhs = left_side(k) if k < 4 else None
            for n in range(CHUNKS):
                if k > 0:
                    weighted = weigh(k - 1, n, highest, weighted)
                if k < 4:
                    top = score(k, n, lhs, top)
            if k > 0:
                mean = weighted[:, 0:HQ] / weighted[:, HQ:]
                attended[gx, (k - 1) * PAIR : k * PAIR, :] = jnp.where(
                    low_head, mean[0:PAIR], mean[PAIR:]
                ).astype(BF16)
                for d in range(XC):
                    go(x_copy(attended_piece(k - 1), 1 + k, d))
            if k < 4:
                highest = jnp.max(top, axis=-1, keepdims=True)

    def finish(part):
        for way in (0, 1):
            if last_step(part, way) == 4:
                ring_copy(part, way, 4, True).wait_recv()

    attend()
    finish(FRONT)
    for copy in front_over_y(4):
        go(copy)
    for n in range(3):
        for d in (1, 3, 2):
            x_pass_on(attended_piece(n), 2 + n, d)

    def wide_row(ref, count):
        return jnp.concatenate([ref[n : n + 1, :] for n in range(count)], axis=1)

    alpha_a = wide_row(alpha_attn, D // HQ)

    def update(k, carry):
        rows = slice(k * PAIR, (k + 1) * PAIR)
        heads = jnp.concatenate([attended[g, rows, :] for g in range(2 * XC)], axis=1)
        out = jnp.concatenate([g_out[g] for g in range(2 * XC)], axis=1)
        mixed = dot_nt(heads, out)
        residual = tokens[rows, :].astype(F32)
        after[rows, :] = rms_unit(residual + alpha_a * (rms_unit(mixed) - residual)).astype(BF16)
        return carry

    for d in range(XC):
        x_from_sibling(out_piece, 1, d)
    for n in range(4):
        for d in range(XC):
            x_from_sibling(attended_piece(n), 2 + n, d)
        update(n, 0)
        if n == 0:
            for d in (1, 3, 2):
                x_pass_on(attended_piece(3), 5, d)
    ring_stage(DOWN, 4)
    ring_stage(REST, 4)

    for n in range(ZC):
        for d in (1, 2, 3):
            piece = l_front.at[lax.rem(z + ZC - n, ZC), from_y(d)]
            remote(
                piece, piece, quarter_send.at[n, d - 1], quarter_recv.at[n, d - 1], along_y[d]
            ).wait_recv()

    def gate_block(b):
        at = b * HQ
        if at < GATE_FRONT:
            return lambda zz, yy: l_front[zz, yy, :, FF + at : FF + at + HQ]
        at -= GATE_FRONT
        return lambda zz, yy: l_rest[zz, yy, :, at : at + HQ]

    def put_up(b):
        def put(rows, value):
            g_ff[b, rows, 0:HQ] = value

        return put

    def put_gate(b):
        def put(rows, value):
            g_ff[b, rows, HQ : 2 * HQ] = value

        return put

    def put_down(rows, value):
        g_down[rows, :] = value

    def assemble_front(p, carry):
        for b in range(FF // HQ):
            assemble(p, lambda zz, yy, b=b: l_front[zz, yy, :, b * HQ : (b + 1) * HQ], put_up(b))
        for b in range(GATE_FRONT // HQ):
            assemble(p, gate_block(b), put_gate(b))
        return carry

    def assemble_rest(p, carry):
        for b in range(GATE_FRONT // HQ, FF // HQ):
            assemble(p, gate_block(b), put_gate(b))
        assemble(p, lambda zz, yy: l_down[zz, yy], put_down)
        return carry

    lax.fori_loop(0, D // (2 * SHARD), assemble_front, 0)
    finish(DOWN)
    finish(REST)
    lax.fori_loop(0, D // (2 * SHARD), assemble_rest, 0)

    s_up_row = wide_row(s_up, FF // HQ)
    s_gate_row = wide_row(s_gate, FF // HQ)

    def far_first(k):
        return jnp.where(k == 0, 2, jnp.where(k == 1, 1, jnp.where(k == 2, 3, 0)))

    def feed(k):
        block = lax.rem(x + far_first(k), XC)
        rows = after[pl.ds(pl.multiple_of(block * PAIR, PAIR), PAIR), :]
        acts = []
        for b in range(5):
            both = dot(rows, g_ff[b])
            cols = slice(b * HQ, b * HQ + HQ)
            up = both[:, 0:HQ] * s_up_row[:, cols]
            gate = both[:, HQ:] * s_gate_row[:, cols]
            acts.append((up * (gate / (1.0 + jnp.exp(-gate)))).astype(BF16))
        active = jnp.concatenate(acts, axis=1)
        partial[...] = dot_nt(active, g_down[...])
        give_halves(k)

    def feed_step(k, carry):
        feed(k)

        @pl.when(k >= 1)
        def _():
            send_sum(k - 1, far_first(k - 1))

        return carry

    lax.fori_loop(0, 4, feed_step, 0)
    lowered = chip_sum(3)
    for k, d in ((0, 2), (1, 1), (2, 3)):
        owner_copy(k, d).wait_recv()
        lowered = lowered + from_peer[k].astype(F32)
    wide = after[block_of(gx), :].astype(F32)
    alpha_m = wide_row(alpha_mlp, D // HQ)
    result[0] = rms_unit(wide + alpha_m * (rms_unit(lowered) - wide)).astype(BF16)

    for copy in sent:
        copy.wait_send()
    for k in range(4):
        sib_copy(k).wait_send()
    for k, d in ((0, 2), (1, 1), (2, 3)):
        owner_copy(k, d).wait_send()


SPAN = TOK + 16


BANDS = 4


def append_kernel(
    lengths, cached, fresh, hidden, new_hidden, new_cycle, cycle, new_rows, own, sem
):
    start = jnp.clip(lax.rem(lengths[0] - SINK, CYCLE), 0, CYCLE - SPAN)
    base = pl.multiple_of(start // 16 * 16, 16)
    shift = start - base
    bands = [(n, b, pl.ds(b * (CYCLE // BANDS), CYCLE // BANDS)) for n in (0, 1) for b in range(BANDS)]
    loads = [pltpu.make_async_copy(cached.at[0, n, r], cycle.at[n, r], sem.at[0, n, b]) for n, b, r in bands]
    stores = [pltpu.make_async_copy(cycle.at[n, r], new_cycle.at[0, n, r], sem.at[1, n, b]) for n, b, r in bands]
    rows_in = pltpu.make_async_copy(fresh.at[0], new_rows, sem.at[2, 0, 0])
    own_in = pltpu.make_async_copy(hidden.at[0], own, sem.at[2, 0, 1])
    own_out = pltpu.make_async_copy(own, new_hidden.at[0], sem.at[2, 0, 2])
    for load in (rows_in, own_in, *loads):
        load.start()
    row = rows_of((SPAN, HQ))
    here = (row >= shift) & (row < shift + TOK)
    rows_in.wait()
    for n in (0, 1):
        rows = jnp.concatenate([new_rows[n].astype(F32), jnp.zeros((16, HQ), F32)], axis=0)
        rows = pltpu.roll(rows, shift, 0)
        if n == 0:
            own_in.wait()
            own_out.start()
        for load in loads[n * BANDS : (n + 1) * BANDS]:
            load.wait()
        window = cycle.at[n, pl.ds(base, SPAN)]
        window[...] = jnp.where(here, rows, window[...].astype(F32)).astype(BF16)
        for store in stores[n * BANDS : (n + 1) * BANDS]:
            store.start()
    for copy in (*stores, own_out):
        copy.wait()


def per_device(
    hidden,
    lengths,
    sink_kv,
    kv_cycle,
    w_qkv,
    s_qk,
    w_out,
    alpha_attn,
    w_up,
    w_gate,
    s_up,
    s_gate,
    w_down,
    alpha_mlp,
):
    vmem = pl.BlockSpec(memory_space=pltpu.VMEM)
    anywhere = pl.BlockSpec(memory_space=pl.ANY)
    dma = pltpu.SemaphoreType.DMA
    result, fresh = pl.pallas_call(
        layer_kernel,
        out_shape=(
            jax.ShapeDtypeStruct((1, OWN, D), BF16),
            jax.ShapeDtypeStruct((1, 2, TOK, HQ), BF16),
        ),
        in_specs=[
            pl.BlockSpec(memory_space=pltpu.SMEM),
            anywhere,
            vmem,
            anywhere,
            anywhere,
            vmem,
            anywhere,
            vmem,
            anywhere,
            anywhere,
            vmem,
            vmem,
            anywhere,
            vmem,
        ],
        out_specs=(vmem, vmem),
        scratch_shapes=[
            pltpu.VMEM((ZC, YC, 3, SHARD, HQ), BF16),
            pltpu.VMEM((ZC, YC, SHARD, HQ), BF16),
            pltpu.VMEM((ZC, YC, SHARD, FF), BF16),
            pltpu.VMEM((ZC, YC, SHARD, GATE_REST), BF16),
            pltpu.VMEM((ZC, YC, SHARD, FF + GATE_FRONT), BF16),
            pltpu.VMEM((D, 3 * HQ), BF16),
            pltpu.VMEM((2 * XC, D, HQ), BF16),
            pltpu.VMEM((5, D, 2 * HQ), BF16),
            pltpu.VMEM((D, FF), BF16),
            pltpu.VMEM((TOK, D), BF16),
            pltpu.VMEM((KEYS, 2 * HQ), BF16),
            pltpu.VMEM((KEYS, 2 * HQ), BF16),
            pltpu.VMEM((TOK, HQ), BF16),
            pltpu.VMEM((2 * PAIR, CHUNK * CHUNKS), F32),
            pltpu.VMEM((2 * PAIR, CHUNK * CHUNKS), F32),
            pltpu.VMEM((2 * XC, TOK, HQ), BF16),
            pltpu.VMEM((PAIR, D), F32),
            pltpu.VMEM((4, OWN, D), F32),
            pltpu.VMEM((4, OWN, D), BF16),
            pltpu.VMEM((4, OWN, D), BF16),
            pltpu.VMEM((4, OWN, D), BF16),
            pltpu.VMEM((4, OWN, D), BF16),
            pltpu.VMEM((TOK, D), BF16),
            dma((11,)),
            dma((6, 7)),
            dma((6, 7)),
            dma((4, ZC)),
            dma((4, ZC)),
            dma((ZC,)),
            dma((ZC,)),
            dma((3, 3)),
            dma((3, 3)),
            dma((3, 2, 4)),
            dma((3, 2, 4)),
            dma((ZC, 3)),
            dma((ZC, 3)),
            dma((4,)),
            dma((4,)),
            dma((4,)),
            dma((4,)),
        ],
        compiler_params=pltpu.CompilerParams(
            collective_id=0, has_side_effects=True, vmem_limit_bytes=56 * 2**20
        ),
    )(
        lengths,
        hidden,
        sink_kv,
        kv_cycle,
        w_qkv.transpose(1, 0, 2),
        s_qk.reshape(1, HQ),
        w_out.T,
        alpha_attn.reshape(D // HQ, HQ),
        w_up,
        w_gate,
        s_up.reshape(FF // HQ, HQ),
        s_gate.reshape(FF // HQ, HQ),
        w_down.T,
        alpha_mlp.reshape(D // HQ, HQ),
    )
    return pl.pallas_call(
        append_kernel,
        out_shape=(
            jax.ShapeDtypeStruct((1, OWN, D), BF16),
            jax.ShapeDtypeStruct(kv_cycle.shape, BF16),
        ),
        in_specs=[pl.BlockSpec(memory_space=pltpu.SMEM), anywhere, anywhere, anywhere],
        out_specs=(anywhere, anywhere),
        scratch_shapes=[
            pltpu.VMEM((2, CYCLE, HQ), BF16),
            pltpu.VMEM((2, TOK, HQ), BF16),
            pltpu.VMEM((OWN, D), BF16),
            dma((3, 2, BANDS)),
        ],
        compiler_params=pltpu.CompilerParams(vmem_limit_bytes=56 * 2**20),
    )(lengths, kv_cycle, fresh, result)


def solution(mesh):
    return jax.shard_map(
        per_device,
        mesh=mesh,
        in_specs=(
            P("gy", "gx", None),
            P("gy"),
            P("gy", None, None, "gx"),
            P("gy", None, None, "gx"),
            P("gy", None, "gx"),
            P("gx"),
            P("gx", "gy"),
            P(),
            P("gy", "gx"),
            P("gy", "gx"),
            P("gx"),
            P("gx"),
            P("gx", "gy"),
            P(),
        ),
        out_specs=(P("gy", "gx", None), P("gy", None, None, "gx")),
        check_vma=False,
    )
```

```python
import functools

import jax
import jax.numpy as jnp
from jax import lax
from jax.experimental import pallas as pl
from jax.experimental.pallas import tpu as pltpu
from jax.sharding import PartitionSpec as P

MESH = pl.DeviceIdType.MESH
BF16 = jnp.bfloat16
F32 = jnp.float32

XC, YC, ZC = 4, 4, 8
D = 1280
HQ = 128
FF = 640
TOK = 512
OWN = 64
PAIR = 128
SHARD = 40
PLANE = SHARD * YC
SINK = 4
WINDOW = 4096
CYCLE = 4608
LONG = 16384
HEAD = 3056
TAIL = 2544
OLD = CYCLE - HEAD + TAIL
NEW_AT = OLD + 16
CHUNK = 256
CHUNKS = 17
KEYS = 3 * PAIR + CHUNK * CHUNKS
FIRST = 13
AWAY = -1e30
DOWN, REST, FRONT = 0, 1, 2
OUT = 2
GATE_FRONT = 256
GATE_REST = FF - GATE_FRONT
RIGHT_LAST = (DOWN,)


def dot(a, b):
    return jnp.dot(a, b, preferred_element_type=F32)


def dot_nt(a, b):
    return lax.dot_general(a, b, (((1,), (1,)), ((), ())), preferred_element_type=F32)


def rms_unit(values):
    return values * lax.rsqrt(jnp.mean(values * values, axis=-1, keepdims=True) + 1e-06)


def lanes(shape):
    return lax.broadcasted_iota(jnp.int32, shape, len(shape) - 1)


def rows_of(shape):
    return lax.broadcasted_iota(jnp.int32, shape, len(shape) - 2)


def layer_kernel(
    lengths,
    hidden,
    sinks,
    cached,
    w_qkv,
    s_qk,
    w_out,
    alpha_attn,
    w_up,
    w_gate,
    s_up,
    s_gate,
    w_down,
    alpha_mlp,
    result,
    fresh,
    l_qkv,
    l_out,
    l_down,
    l_rest,
    l_front,
    g_qkv,
    g_out,
    g_ff,
    g_down,
    tokens,
    keys,
    values,
    queries,
    even_scores,
    odd_scores,
    attended,
    partial,
    kept,
    to_sib,
    from_sib,
    to_owner,
    from_peer,
    after,
    local_sem,
    tok_send,
    tok_recv,
    qkv_send,
    qkv_recv,
    out_send,
    out_recv,
    shard_send,
    shard_recv,
    ring_send,
    ring_recv,
    quarter_send,
    quarter_recv,
    sib_send,
    sib_recv,
    sum_send,
    sum_recv,
):
    gx = lax.axis_index("gx")
    gy = lax.axis_index("gy")
    x, c = gx // 2, lax.rem(gx, 2)
    z, y = gy // YC, lax.rem(gy, YC)

    def device(dx=0, other=False, dz=0, dy=0):
        core = 1 - c if other else c
        return (
            lax.rem(x + dx, XC) * 2 + core,
            lax.rem(z + dz, ZC) * YC + lax.rem(y + dy, YC),
        )

    sibling = device(other=True)
    along_x = {d: device(dx=d) for d in (1, 2, 3)}
    along_y = {d: device(dy=d) for d in (1, 2, 3)}
    right, left = device(dz=1), device(dz=ZC - 1)
    along_z = [device(dz=d) for d in range(1, ZC)]
    everyone = [sibling, *along_x.values(), *along_y.values(), *along_z]
    gate_sem = pltpu.get_barrier_semaphore()
    for peer in everyone:
        pl.semaphore_signal(gate_sem, inc=1, device_id=peer, device_id_type=MESH)

    sent = []

    def remote(src, dst, send, recv, to):
        return pltpu.make_async_remote_copy(
            src_ref=src, dst_ref=dst, send_sem=send, recv_sem=recv, device_id=to, device_id_type=MESH
        )

    def go(copy):
        copy.start()
        sent.append(copy)

    def block_of(g):
        return pl.ds(pl.multiple_of(g * OWN, OWN), OWN)

    own_in = pltpu.make_async_copy(hidden.at[0], tokens.at[block_of(gx)], local_sem.at[0])
    own_in.start()
    loads = []
    for kind, store in ((0, keys), (1, values)):
        for n, (src, at, count) in enumerate(
            ((HEAD, 0, CYCLE - HEAD), (0, CYCLE - HEAD, TAIL + 16))
        ):
            loads.append(
                pltpu.make_async_copy(
                    cached.at[0, kind, pl.ds(src, count)],
                    store.at[pl.ds(at, count), pl.ds(0, HQ)],
                    local_sem.at[1 + 2 * kind + n],
                )
            )
    for load in loads:
        load.start()

    mine = [
        (w_qkv, l_qkv.at[z, y]),
        (w_up, l_front.at[z, y, :, pl.ds(0, FF)]),
        (w_gate.at[:, pl.ds(0, GATE_FRONT)], l_front.at[z, y, :, pl.ds(FF, GATE_FRONT)]),
        (w_gate.at[:, pl.ds(GATE_FRONT, GATE_REST)], l_rest.at[z, y, :, pl.ds(0, GATE_REST)]),
        (w_down, l_down.at[z, y]),
        (w_out, l_out.at[z, y]),
    ]
    mine = [pltpu.make_async_copy(a, b, local_sem.at[5 + n]) for n, (a, b) in enumerate(mine)]
    for copy in mine:
        copy.start()

    def over_y(piece, sends, recvs):
        return [remote(piece, piece, sends(d - 1), recvs(d - 1), along_y[d]) for d in (1, 2, 3)]

    def qkv_over_z(dz, arriving=False):
        zz = lax.rem(z + ZC - dz, ZC) if arriving else z
        piece = l_qkv.at[zz, y]
        return remote(piece, piece, qkv_send.at[0, dz], qkv_recv.at[0, dz], device(dz=dz))

    def qkv_over_y(dz):
        piece = l_qkv.at[lax.rem(z + ZC - dz, ZC), y]
        return over_y(piece, lambda n: qkv_send.at[1 + n, dz], lambda n: qkv_recv.at[1 + n, dz])

    def out_over_z(dz, arriving=False):
        piece = l_out.at[lax.rem(z + ZC - dz, ZC) if arriving else z]
        return remote(piece, piece, out_send.at[dz], out_recv.at[dz], device(dz=dz))

    def from_y(d):
        return lax.rem(y + YC - d, YC)

    def shard_over_y(part):
        piece = (l_down, l_rest, l_out)[part].at[z, y]
        return over_y(piece, lambda n: shard_send.at[part, n], lambda n: shard_recv.at[part, n])

    def shard_arrived(part):
        for d in (1, 2, 3):
            piece = (l_down, l_rest, l_out)[part].at[z, from_y(d)]
            remote(
                piece, piece, shard_send.at[part, d - 1], shard_recv.at[part, d - 1], along_y[d]
            ).wait_recv()

    def last_step(part, way):
        return 4 if (part in RIGHT_LAST) == (way == 0) else 3

    def ring_copy(part, way, step, arriving):
        back = step if arriving else step - 1
        zz = lax.rem(z + ZC - back, ZC) if way == 0 else lax.rem(z + back, ZC)
        piece = (l_down.at[zz], l_rest.at[zz], l_front.at[zz, y])[part]
        return remote(
            piece,
            piece,
            ring_send.at[part, way, step - 1],
            ring_recv.at[part, way, step - 1],
            right if way == 0 else left,
        )

    def front_over_y(n):
        piece = l_front.at[lax.rem(z + ZC - n, ZC), y]
        return over_y(piece, lambda m: quarter_send.at[n, m], lambda m: quarter_recv.at[n, m])

    def ring_stage(part, step):
        for way in (0, 1):
            if 1 <= step - 1 <= last_step(part, way):
                ring_copy(part, way, step - 1, True).wait_recv()
            if step <= last_step(part, way):
                go(ring_copy(part, way, step, False))

    pl.semaphore_wait(gate_sem, len(everyone))
    mine[0].wait()
    for dz in (1, 7, 2, 6, 3, 5, 4):
        go(qkv_over_z(dz))
    mine[5].wait()
    for copy in (*shard_over_y(OUT), *qkv_over_y(0)):
        go(copy)
    for n in (3, 4):
        mine[n].wait()
    for part in (DOWN, REST):
        for copy in shard_over_y(part):
            go(copy)

    own_in.wait()

    def held_by(d, other=False):
        core = 1 - c if other else c
        return lax.rem(x + XC - d, XC) * 2 + core

    def token_piece(g):
        return tokens.at[block_of(g)]

    def out_piece(g):
        return g_out.at[g]

    def attended_piece(n):
        return lambda g: attended.at[g, pl.ds(pl.multiple_of(n * PAIR, PAIR), PAIR)]

    def x_copy(piece, phase, d):
        to = sibling if d == 0 else along_x[d]
        return remote(piece(gx), piece(gx), tok_send.at[phase, d], tok_recv.at[phase, d], to)

    def x_pass_copy(piece, phase, d):
        block = piece(held_by(d))
        return remote(block, block, tok_send.at[phase, 3 + d], tok_recv.at[phase, 3 + d], sibling)

    def x_pass_on(piece, phase, d):
        block = piece(held_by(d))
        remote(
            block, block, tok_send.at[phase, d], tok_recv.at[phase, d], along_x[d]
        ).wait_recv()
        go(x_pass_copy(piece, phase, d))

    def x_from_sibling(piece, phase, d):
        block = piece(held_by(d, True))
        n = 0 if d == 0 else 3 + d
        remote(block, block, tok_send.at[phase, n], tok_recv.at[phase, n], sibling).wait_recv()

    for d in (1, 3, 2, 0):
        go(x_copy(token_piece, 0, d))

    for n in (1, 2):
        mine[n].wait()
    ring_stage(FRONT, 1)

    def pass_on_qkv(dz):
        qkv_over_z(dz, True).wait_recv()
        for copy in qkv_over_y(dz):
            go(copy)

    for dz in (1, 7, 2, 6):
        pass_on_qkv(dz)
    shard_arrived(OUT)
    for dz in (1, 7, 2, 6, 3, 5, 4):
        go(out_over_z(dz))
    for dz in (3, 5, 4):
        pass_on_qkv(dz)
    for part in (DOWN, REST):
        shard_arrived(part)
        ring_stage(part, 1)

    length = lengths[0]

    def key_bias(n, carry):
        at = pl.multiple_of(n * PAIR, PAIR)
        row = rows_of((PAIR, HQ)) + at
        slot = jnp.where(row < CYCLE - HEAD, row + HEAD, row - (CYCLE - HEAD))
        lag = length - 1 - SINK - slot
        turns = (
            jnp.where(lag >= CYCLE, 1, 0)
            + jnp.where(lag >= 2 * CYCLE, 1, 0)
            + jnp.where(lag >= 3 * CYCLE, 1, 0)
        )
        held = SINK + slot + CYCLE * turns
        old = (lag >= 0) & (held >= length - WINDOW) & (row < OLD + 12)
        seen = old | ((row >= OLD + 12) & (row < NEW_AT + TOK))
        keys[pl.ds(at, PAIR), HQ : 2 * HQ] = jnp.where(seen, 0.0, AWAY).astype(BF16)
        values[pl.ds(at, PAIR), HQ : 2 * HQ] = jnp.ones((PAIR, HQ), BF16)
        return carry

    lax.fori_loop(0, KEYS // PAIR, key_bias, 0)
    spare = KEYS - NEW_AT - TOK
    for load in loads:
        load.wait()
    tile_row = rows_of((16, HQ))
    for kind, store in ((0, keys), (1, values)):
        store[NEW_AT + TOK :, 0:HQ] = jnp.zeros((spare, HQ), BF16)
        tile = store[OLD:NEW_AT, 0:HQ].astype(F32)
        sink_rows = sinks[0, kind].astype(F32)
        for r in range(SINK):
            tile = jnp.where(tile_row == 12 + r, sink_rows[r : r + 1], tile)
        store[OLD:NEW_AT, 0:HQ] = tile.astype(BF16)

    for d in (1, 3, 2):
        x_pass_on(token_piece, 0, d)

    def assemble(p, take, put):
        zz, pair = p // 2, lax.rem(p, 2)
        low, high = take(zz, 2 * pair), take(zz, 2 * pair + 1)
        put(
            pl.ds(pl.multiple_of(p * 2 * SHARD, 16), 2 * SHARD),
            jnp.concatenate([low.astype(F32), high.astype(F32)], axis=0).astype(BF16),
        )

    def put_out(rows, value):
        g_out[gx, rows, :] = value

    def assemble_out(p, carry):
        assemble(p, lambda zz, yy: l_out[zz, yy], put_out)
        return carry

    for dz in (1, 7, 2, 6, 3, 5, 4):
        out_over_z(dz, True).wait_recv()
    lax.fori_loop(0, D // (2 * SHARD), assemble_out, 0)
    for d in (2, 1, 3, 0):
        go(x_copy(out_piece, 1, d))
    ring_stage(FRONT, 2)
    for n in range(ZC):
        for d in (1, 2, 3):
            piece = l_qkv.at[lax.rem(z + ZC - n, ZC), from_y(d)]
            remote(
                piece, piece, qkv_send.at[d, n], qkv_recv.at[d, n], along_y[d]
            ).wait_recv()
    ring_stage(DOWN, 2)
    ring_stage(REST, 2)
    for n in (0, 1, 7):
        for copy in front_over_y(n):
            go(copy)

    def assemble_qkv(p, carry):
        for n in range(3):

            def put(rows, value, n=n):
                g_qkv[rows, n * HQ : (n + 1) * HQ] = value

            assemble(p, lambda zz, yy, n=n: l_qkv[zz, yy, n], put)
        return carry

    lax.fori_loop(0, D // (2 * SHARD), assemble_qkv, 0)
    for d in (0, 1, 2, 3):
        x_from_sibling(token_piece, 0, d)

    low_head = lanes((PAIR, HQ)) < 64

    def head_unit(v):
        squares = v * v
        low = jnp.sum(jnp.where(low_head, squares, 0.0), axis=-1, keepdims=True)
        high = jnp.sum(jnp.where(low_head, 0.0, squares), axis=-1, keepdims=True)
        return v * jnp.where(low_head, lax.rsqrt(low + 1e-06), lax.rsqrt(high + 1e-06))

    def project(n, carry):
        at = pl.multiple_of(n * PAIR, PAIR)
        qkv = dot(tokens[pl.ds(at, PAIR), :], g_qkv[...])
        scale = s_qk[...]
        q = (head_unit(qkv[:, 0:HQ]) * scale).astype(BF16)
        queries[pl.ds(at, PAIR), :] = (q.astype(F32) * 8.0).astype(BF16)
        k = (head_unit(qkv[:, HQ : 2 * HQ]) * scale).astype(BF16)
        v = qkv[:, 2 * HQ :].astype(BF16)
        to = pl.ds(pl.multiple_of(NEW_AT + at, 16), PAIR)
        keys[to, 0:HQ] = k
        values[to, 0:HQ] = v
        fresh[0, 0, pl.ds(at, PAIR), :] = k
        fresh[0, 1, pl.ds(at, PAIR), :] = v
        return carry

    lax.fori_loop(0, TOK // PAIR, project, 0)
    ring_stage(FRONT, 3)
    for n in (2, 6):
        for copy in front_over_y(n):
            go(copy)

    def own_half(ref):
        return ref[pl.ds(pl.multiple_of(c * OWN, OWN), OWN), :]

    def other_half(ref):
        return ref[pl.ds(pl.multiple_of((1 - c) * OWN, OWN), OWN), :]

    def sib_copy(k):
        return remote(
            to_sib.at[k],
            from_sib.at[k],
            sib_send.at[k],
            sib_recv.at[k],
            sibling,
        )

    def owner_copy(k, d):
        to = (lax.rem(x + d, XC) * 2 + c, gy)
        return remote(
            to_owner.at[k],
            from_peer.at[k],
            sum_send.at[k],
            sum_recv.at[k],
            to,
        )

    def give_halves(k):
        kept[k] = own_half(partial)
        to_sib[k] = other_half(partial).astype(BF16)
        sib_copy(k).start()

    def chip_sum(k):
        sib_copy(k).wait_recv()
        return kept[k] + from_sib[k].astype(F32)

    def send_sum(k, d):
        to_owner[k] = chip_sum(k).astype(BF16)
        owner_copy(k, d).start()

    query_row = jnp.where(
        rows_of((2 * PAIR, CHUNK)) >= PAIR, rows_of((2 * PAIR, CHUNK)) - PAIR, rows_of((2 * PAIR, CHUNK))
    )
    key_col = lanes((2 * PAIR, CHUNK))

    def left_side(k):
        q = queries[k * PAIR : (k + 1) * PAIR, :]
        zero = jnp.zeros_like(q)
        both = jnp.concatenate([jnp.where(low_head, q, zero), jnp.where(low_head, zero, q)], axis=0)
        return jnp.concatenate([both, jnp.ones((2 * PAIR, HQ), BF16)], axis=1)

    def score(k, n, lhs, top):
        s = dot_nt(lhs, keys[k * PAIR + n * CHUNK : k * PAIR + (n + 1) * CHUNK, :])
        if n == 0:
            s = jnp.where(key_col >= query_row + FIRST, s, AWAY)
        if n == CHUNKS - 1:
            s = jnp.where(key_col + n * CHUNK <= query_row + NEW_AT, s, AWAY)
        (even_scores, odd_scores)[k % 2][:, n * CHUNK : (n + 1) * CHUNK] = s
        part = jnp.maximum(s[:, 0:HQ], s[:, HQ:])
        return part if top is None else jnp.maximum(top, part)

    def weigh(k, n, highest, weighted):
        s = (even_scores, odd_scores)[k % 2][:, n * CHUNK : (n + 1) * CHUNK]
        w = jnp.exp(s - highest).astype(BF16)
        part = dot(w, values[k * PAIR + n * CHUNK : k * PAIR + (n + 1) * CHUNK, :])
        return part if weighted is None else weighted + part

    def attend():
        highest = None
        for k in range(5):
            if k == 2:
                ring_stage(FRONT, 4)
                for n in (3, 5):
                    for copy in front_over_y(n):
                        go(copy)
            if k == 4:
                for d in (1, 3, 2):
                    x_pass_on(out_piece, 1, d)
            if k == 3:
                ring_stage(DOWN, 3)
                ring_stage(REST, 3)
            top, weighted = None, None
            lhs = left_side(k) if k < 4 else None
            for n in range(CHUNKS):
                if k > 0:
                    weighted = weigh(k - 1, n, highest, weighted)
                if k < 4:
                    top = score(k, n, lhs, top)
            if k > 0:
                mean = weighted[:, 0:HQ] / weighted[:, HQ:]
                attended[gx, (k - 1) * PAIR : k * PAIR, :] = jnp.where(
                    low_head, mean[0:PAIR], mean[PAIR:]
                ).astype(BF16)
                for d in range(XC):
                    go(x_copy(attended_piece(k - 1), 1 + k, d))
            if k < 4:
                highest = jnp.max(top, axis=-1, keepdims=True)

    def finish(part):
        for way in (0, 1):
            if last_step(part, way) == 4:
                ring_copy(part, way, 4, True).wait_recv()

    attend()
    finish(FRONT)
    for copy in front_over_y(4):
        go(copy)
    for n in range(3):
        for d in (1, 3, 2):
            x_pass_on(attended_piece(n), 2 + n, d)

    def wide_row(ref, count):
        return jnp.concatenate([ref[n : n + 1, :] for n in range(count)], axis=1)

    alpha_a = wide_row(alpha_attn, D // HQ)

    def update(k, carry):
        rows = slice(k * PAIR, (k + 1) * PAIR)
        heads = jnp.concatenate([attended[g, rows, :] for g in range(2 * XC)], axis=1)
        out = jnp.concatenate([g_out[g] for g in range(2 * XC)], axis=1)
        mixed = dot_nt(heads, out)
        residual = tokens[rows, :].astype(F32)
        after[rows, :] = rms_unit(residual + alpha_a * (rms_unit(mixed) - residual)).astype(BF16)
        return carry

    for d in range(XC):
        x_from_sibling(out_piece, 1, d)
    for n in range(4):
        for d in range(XC):
            x_from_sibling(attended_piece(n), 2 + n, d)
        update(n, 0)
        if n == 0:
            for d in (1, 3, 2):
                x_pass_on(attended_piece(3), 5, d)
        if n == 0:
            ring_stage(DOWN, 4)
            ring_stage(REST, 4)

    for n in range(ZC):
        for d in (1, 2, 3):
            piece = l_front.at[lax.rem(z + ZC - n, ZC), from_y(d)]
            remote(
                piece, piece, quarter_send.at[n, d - 1], quarter_recv.at[n, d - 1], along_y[d]
            ).wait_recv()

    def gate_block(b):
        at = b * HQ
        if at < GATE_FRONT:
            return lambda zz, yy: l_front[zz, yy, :, FF + at : FF + at + HQ]
        at -= GATE_FRONT
        return lambda zz, yy: l_rest[zz, yy, :, at : at + HQ]

    def put_up(b):
        def put(rows, value):
            g_ff[b, rows, 0:HQ] = value

        return put

    def put_gate(b):
        def put(rows, value):
            g_ff[b, rows, HQ : 2 * HQ] = value

        return put

    def put_down(rows, value):
        g_down[rows, :] = value

    def assemble_front(p, carry):
        for b in range(FF // HQ):
            assemble(p, lambda zz, yy, b=b: l_front[zz, yy, :, b * HQ : (b + 1) * HQ], put_up(b))
        for b in range(GATE_FRONT // HQ):
            assemble(p, gate_block(b), put_gate(b))
        return carry

    def assemble_rest(p, carry):
        for b in range(GATE_FRONT // HQ, FF // HQ):
            assemble(p, gate_block(b), put_gate(b))
        assemble(p, lambda zz, yy: l_down[zz, yy], put_down)
        return carry

    lax.fori_loop(0, D // (2 * SHARD), assemble_front, 0)
    finish(DOWN)
    finish(REST)
    lax.fori_loop(0, D // (2 * SHARD), assemble_rest, 0)

    s_up_row = wide_row(s_up, FF // HQ)
    s_gate_row = wide_row(s_gate, FF // HQ)

    def far_first(k):
        return jnp.where(k == 0, 2, jnp.where(k == 1, 1, jnp.where(k == 2, 3, 0)))

    def feed(k):
        block = lax.rem(x + far_first(k), XC)
        rows = after[pl.ds(pl.multiple_of(block * PAIR, PAIR), PAIR), :]
        acts = []
        for b in range(5):
            both = dot(rows, g_ff[b])
            cols = slice(b * HQ, b * HQ + HQ)
            up = both[:, 0:HQ] * s_up_row[:, cols]
            gate = both[:, HQ:] * s_gate_row[:, cols]
            acts.append((up * (gate / (1.0 + jnp.exp(-gate)))).astype(BF16))
        active = jnp.concatenate(acts, axis=1)
        partial[...] = dot_nt(active, g_down[...])
        give_halves(k)

    def feed_step(k, carry):
        feed(k)

        @pl.when(k >= 1)
        def _():
            send_sum(k - 1, far_first(k - 1))

        return carry

    lax.fori_loop(0, 4, feed_step, 0)
    lowered = chip_sum(3)
    for k, d in ((0, 2), (1, 1), (2, 3)):
        owner_copy(k, d).wait_recv()
        lowered = lowered + from_peer[k].astype(F32)
    wide = after[block_of(gx), :].astype(F32)
    alpha_m = wide_row(alpha_mlp, D // HQ)
    result[0] = rms_unit(wide + alpha_m * (rms_unit(lowered) - wide)).astype(BF16)

    for copy in sent:
        copy.wait_send()
    for k in range(4):
        sib_copy(k).wait_send()
    for k, d in ((0, 2), (1, 1), (2, 3)):
        owner_copy(k, d).wait_send()


SPAN = TOK + 16


BANDS = 4


def append_kernel(
    lengths, cached, fresh, hidden, new_hidden, new_cycle, cycle, new_rows, own, sem
):
    start = jnp.clip(lax.rem(lengths[0] - SINK, CYCLE), 0, CYCLE - SPAN)
    base = pl.multiple_of(start // 16 * 16, 16)
    shift = start - base
    bands = [(n, b, pl.ds(b * (CYCLE // BANDS), CYCLE // BANDS)) for n in (0, 1) for b in range(BANDS)]
    loads = [pltpu.make_async_copy(cached.at[0, n, r], cycle.at[n, r], sem.at[0, n, b]) for n, b, r in bands]
    stores = [pltpu.make_async_copy(cycle.at[n, r], new_cycle.at[0, n, r], sem.at[1, n, b]) for n, b, r in bands]
    rows_in = pltpu.make_async_copy(fresh.at[0], new_rows, sem.at[2, 0, 0])
    own_in = pltpu.make_async_copy(hidden.at[0], own, sem.at[2, 0, 1])
    own_out = pltpu.make_async_copy(own, new_hidden.at[0], sem.at[2, 0, 2])
    for load in (rows_in, own_in, *loads):
        load.start()
    row = rows_of((SPAN, HQ))
    here = (row >= shift) & (row < shift + TOK)
    rows_in.wait()
    for n in (0, 1):
        rows = jnp.concatenate([new_rows[n].astype(F32), jnp.zeros((16, HQ), F32)], axis=0)
        rows = pltpu.roll(rows, shift, 0)
        if n == 0:
            own_in.wait()
            own_out.start()
        for load in loads[n * BANDS : (n + 1) * BANDS]:
            load.wait()
        window = cycle.at[n, pl.ds(base, SPAN)]
        window[...] = jnp.where(here, rows, window[...].astype(F32)).astype(BF16)
        for store in stores[n * BANDS : (n + 1) * BANDS]:
            store.start()
    for copy in (*stores, own_out):
        copy.wait()


def per_device(
    hidden,
    lengths,
    sink_kv,
    kv_cycle,
    w_qkv,
    s_qk,
    w_out,
    alpha_attn,
    w_up,
    w_gate,
    s_up,
    s_gate,
    w_down,
    alpha_mlp,
):
    vmem = pl.BlockSpec(memory_space=pltpu.VMEM)
    anywhere = pl.BlockSpec(memory_space=pl.ANY)
    dma = pltpu.SemaphoreType.DMA
    result, fresh = pl.pallas_call(
        layer_kernel,
        out_shape=(
            jax.ShapeDtypeStruct((1, OWN, D), BF16),
            jax.ShapeDtypeStruct((1, 2, TOK, HQ), BF16),
        ),
        in_specs=[
            pl.BlockSpec(memory_space=pltpu.SMEM),
            anywhere,
            vmem,
            anywhere,
            anywhere,
            vmem,
            anywhere,
            vmem,
            anywhere,
            anywhere,
            vmem,
            vmem,
            anywhere,
            vmem,
        ],
        out_specs=(vmem, vmem),
        scratch_shapes=[
            pltpu.VMEM((ZC, YC, 3, SHARD, HQ), BF16),
            pltpu.VMEM((ZC, YC, SHARD, HQ), BF16),
            pltpu.VMEM((ZC, YC, SHARD, FF), BF16),
            pltpu.VMEM((ZC, YC, SHARD, GATE_REST), BF16),
            pltpu.VMEM((ZC, YC, SHARD, FF + GATE_FRONT), BF16),
            pltpu.VMEM((D, 3 * HQ), BF16),
            pltpu.VMEM((2 * XC, D, HQ), BF16),
            pltpu.VMEM((5, D, 2 * HQ), BF16),
            pltpu.VMEM((D, FF), BF16),
            pltpu.VMEM((TOK, D), BF16),
            pltpu.VMEM((KEYS, 2 * HQ), BF16),
            pltpu.VMEM((KEYS, 2 * HQ), BF16),
            pltpu.VMEM((TOK, HQ), BF16),
            pltpu.VMEM((2 * PAIR, CHUNK * CHUNKS), F32),
            pltpu.VMEM((2 * PAIR, CHUNK * CHUNKS), F32),
            pltpu.VMEM((2 * XC, TOK, HQ), BF16),
            pltpu.VMEM((PAIR, D), F32),
            pltpu.VMEM((4, OWN, D), F32),
            pltpu.VMEM((4, OWN, D), BF16),
            pltpu.VMEM((4, OWN, D), BF16),
            pltpu.VMEM((4, OWN, D), BF16),
            pltpu.VMEM((4, OWN, D), BF16),
            pltpu.VMEM((TOK, D), BF16),
            dma((11,)),
            dma((6, 7)),
            dma((6, 7)),
            dma((4, ZC)),
            dma((4, ZC)),
            dma((ZC,)),
            dma((ZC,)),
            dma((3, 3)),
            dma((3, 3)),
            dma((3, 2, 4)),
            dma((3, 2, 4)),
            dma((ZC, 3)),
            dma((ZC, 3)),
            dma((4,)),
            dma((4,)),
            dma((4,)),
            dma((4,)),
        ],
        compiler_params=pltpu.CompilerParams(
            collective_id=0, has_side_effects=True, vmem_limit_bytes=56 * 2**20
        ),
    )(
        lengths,
        hidden,
        sink_kv,
        kv_cycle,
        w_qkv.transpose(1, 0, 2),
        s_qk.reshape(1, HQ),
        w_out.T,
        alpha_attn.reshape(D // HQ, HQ),
        w_up,
        w_gate,
        s_up.reshape(FF // HQ, HQ),
        s_gate.reshape(FF // HQ, HQ),
        w_down.T,
        alpha_mlp.reshape(D // HQ, HQ),
    )
    return pl.pallas_call(
        append_kernel,
        out_shape=(
            jax.ShapeDtypeStruct((1, OWN, D), BF16),
            jax.ShapeDtypeStruct(kv_cycle.shape, BF16),
        ),
        in_specs=[pl.BlockSpec(memory_space=pltpu.SMEM), anywhere, anywhere, anywhere],
        out_specs=(anywhere, anywhere),
        scratch_shapes=[
            pltpu.VMEM((2, CYCLE, HQ), BF16),
            pltpu.VMEM((2, TOK, HQ), BF16),
            pltpu.VMEM((OWN, D), BF16),
            dma((3, 2, BANDS)),
        ],
        compiler_params=pltpu.CompilerParams(vmem_limit_bytes=56 * 2**20),
    )(lengths, kv_cycle, fresh, result)


def solution(mesh):
    return jax.shard_map(
        per_device,
        mesh=mesh,
        in_specs=(
            P("gy", "gx", None),
            P("gy"),
            P("gy", None, None, "gx"),
            P("gy", None, None, "gx"),
            P("gy", None, "gx"),
            P("gx"),
            P("gx", "gy"),
            P(),
            P("gy", "gx"),
            P("gy", "gx"),
            P("gx"),
            P("gx"),
            P("gx", "gy"),
            P(),
        ),
        out_specs=(P("gy", "gx", None), P("gy", None, None, "gx")),
        check_vma=False,
    )
```
